32 devices in a mesh: basin: 4 (over y, x), blk: 8 (over z, core).
Axes of the slice: x: 2, y: 2, z: 4, core: 2. Of those that a mesh axis runs over, the one named last changes fastest.
Arguments:
- terminal: float32 [64, 128, 128], P(('basin', 'blk')), may hold values from -6 to 6
- depth: float32 [64, 128, 128], P(('basin', 'blk')), may hold values from 1.5 to 4.5
- wet_cells: int32 [64, 128, 128], P(('basin', 'blk')), may hold values from 0 to 1
- neighbours: int32 [64, 4], P(('basin', 'blk')), may hold values from -1 to 63, as said below
- gauge_cell: int32 [1024], P(('basin', 'blk')), may hold values from 0 to 32767
- misfit: float32 [4, 1024], P(None, ('basin', 'blk')), may hold values from -6 to 6
- basis: float32 [64, 4, 128, 128], P(('basin', 'blk')), may hold values from -0.046875 to 0.046875
- subfault_index: int32 [64, 4], P(('basin', 'blk')), may hold values from 0 to 255, as said below
- source: float32 [256], P(('basin', 'blk')), may hold values from -6 to 6
- background: float32 [256], P(('basin', 'blk')), may hold values from -6 to 6
- step_size: float32 [1], replicated, may hold values from 0.25 to 1
Outputs:
- surface: float32 [64, 128, 128], P(('basin', 'blk'))
- updated: float32 [256], P(('basin', 'blk'))
The draws below stay inside these ranges and needn't reach their ends.
Inputs may be any that keep to these rules, and one draw needn't show every extreme that they name: `neighbours`: entry (s, side) is the global slot (device index along basin+blk times 2 plus slot) of the wet block beside slot s's block on the west, east, south or north side, or -1 where that block is dry or off the grid. The relation is mutual: if slot a names b on the west, b names a on the east, and likewise south and north. A named slot lies on a device of the same basin index or of the basin index one lower or higher, wrapping around. Of one device's rows, at most 2 entries name slots of any one other device, and some pair of devices reaches 2. `subfault_index`: A subfault's deformation spans several blocks: every subfault that is named at all is named by two or more entries, in one slot's row or in several.
All inputs are finite; a program needn't handle non-finite values.
Results may differ from the reference program's by a relative error of at most 0.000059.
Values sent between devices are 32-bit elements; how exact they have to be, the bound alone decides.
A program may use at most 64 MiB of HBM per device.

```python
import math
import jax
import jax.numpy as jnp
from jax import lax

BLOCK_CELLS = 128
BPD = 2
COLS = 4
STEPS = 4
G = 32
PATTERNS_PER_SLOT = 4
SUBFAULT_TOTAL = 256
WET_SLOT_TOTAL = 64
GX = 16
GY = 4
N_BASIN = 4
N_BLK = 8
DEVICES = 32


def group_of_column(column):
    return column % 2 * (COLS // 2) + column // 2


def column_of_group(group):
    return group % (COLS // 2) * 2 + group // (COLS // 2)


def block_layout(key):
    group_count = GY * COLS // BPD
    region_count = GX // COLS
    device_count = WET_SLOT_TOTAL // BPD
    per_column = GY // BPD
    grid_rows = 2 * GY
    score_key = jax.random.fold_in(key, 701)
    scores = jax.random.randint(score_key, (GX, grid_rows), 0, 4096) * grid_rows + jnp.arange(grid_rows)[None, :]
    order = jnp.argsort(scores, axis=1)
    chosen = jnp.sort(order[:, :GY], axis=1).astype(jnp.int32)
    chosen = chosen.reshape(GX // COLS, COLS, GY)
    chosen = chosen.at[:, 1, :].set(chosen[:, 0, :])
    chosen = chosen.reshape(GX, GY)
    column_numbers = jnp.arange(GX)[:, None]
    wet_grid = jnp.zeros((GX, grid_rows), jnp.int32).at[column_numbers, chosen].set(1) > 0
    place_grid = jnp.zeros((GX, grid_rows), jnp.int32).at[column_numbers, chosen].set(jnp.arange(GY, dtype=jnp.int32)[None, :])
    member_scores = jax.random.randint(jax.random.fold_in(key, 705), (region_count, group_count), 0, 4096) * group_count + jnp.arange(group_count)[None, :]
    to_physical = jnp.argsort(member_scores, axis=1).astype(jnp.int32)
    region_rows = jnp.arange(region_count)[:, None]
    to_logical = jnp.zeros((region_count, group_count), jnp.int32).at[region_rows, to_physical].set(jnp.arange(group_count, dtype=jnp.int32)[None, :])
    rotation = jax.random.randint(jax.random.fold_in(key, 707), (device_count,), 0, BPD).astype(jnp.int32)
    slot_indices = jnp.arange(WET_SLOT_TOTAL)
    device = slot_indices // BPD
    within = slot_indices % BPD
    region = device // group_count
    physical = device % group_count
    logical = to_logical[region, physical]
    within_logical = (within + rotation[device]) % BPD
    column = column_of_group(logical // per_column)
    position = logical % per_column * BPD + within_logical
    coord_x = region * COLS + column
    coord_y = chosen[coord_x, position]

    def slot_of(place_x, place_y):
        wrapped = place_x % GX
        region_at = wrapped // COLS
        column_at = group_of_column(wrapped % COLS)
        place = place_grid[wrapped, place_y]
        logical_at = column_at * per_column + place // BPD
        device_at = region_at * group_count + to_physical[region_at, logical_at]
        within_at = (place % BPD - rotation[device_at]) % BPD
        return device_at * BPD + within_at
    listed = []
    for step_x, step_y in ((-1, 0), (1, 0), (0, -1), (0, 1)):
        near_x = coord_x + step_x
        near_y = coord_y + step_y
        inside = (near_y >= 0) & (near_y < grid_rows)
        clipped_y = jnp.clip(near_y, 0, grid_rows - 1)
        there = wet_grid[near_x % GX, clipped_y] & inside
        listed.append(jnp.where(there, slot_of(near_x, clipped_y), -1))
    return jnp.stack(listed, axis=1).astype(jnp.int32)


def draw_neighbours(key, part):
    return block_layout(key)


def draw_wet_cells(key, part):
    cell_grid = jax.random.randint(jax.random.fold_in(key, 703), (WET_SLOT_TOTAL, BLOCK_CELLS, BLOCK_CELLS), 0, 100) < 85
    return cell_grid.astype(jnp.int32)


def draw_subfault_index(key, part):
    entry_count = WET_SLOT_TOTAL * PATTERNS_PER_SLOT
    used_count = min(SUBFAULT_TOTAL - 1, entry_count * 2 // 5)
    numbers = jnp.arange(SUBFAULT_TOTAL, dtype=jnp.int32)
    ranking = jax.random.randint(jax.random.fold_in(key, 709), (SUBFAULT_TOTAL,), 0, 4096) * SUBFAULT_TOTAL + numbers
    forced = (numbers == 0) | (numbers == SUBFAULT_TOTAL - 1)
    ranking = jnp.where(forced, -1 - numbers, ranking)
    chosen = jnp.argsort(ranking)[:used_count].astype(jnp.int32)
    listed = chosen[jnp.arange(entry_count) % used_count]
    mixing = jax.random.permutation(jax.random.fold_in(key, 711), entry_count)
    return listed[mixing].reshape(WET_SLOT_TOTAL, PATTERNS_PER_SLOT).astype(jnp.int32)


def with_ends(drawn, key, smallest, high):
    spot = [jax.random.randint(jax.random.fold_in(key, axis), (), 0, length) for axis, length in enumerate(drawn.shape)]
    main_axis = drawn.shape.index(max(drawn.shape))
    beside = spot[:main_axis] + [(spot[main_axis] + 1) % drawn.shape[main_axis]] + spot[main_axis + 1:]
    return drawn.at[tuple(spot)].set(smallest).at[tuple(beside)].set(high)


def shard_levels(own_key, shape, cuts, least, high):
    def one(axis_at, blocks):
        draws = jax.random.uniform(jax.random.fold_in(jax.random.fold_in(own_key, 6), axis_at), (blocks,), jnp.float32, least / len(cuts), high / len(cuts))
        return jnp.repeat(jnp.exp(draws), shape[axis_at] // blocks).reshape((-1,) + (1,) * (len(shape) - axis_at - 1))

    gain = one(*cuts[0])
    for cut in cuts[1:]:
        gain = gain * one(*cut)
    return gain


def scatter_about(rng, dims, deviation, most, cuts=(), kind=jnp.bfloat16):
    values = jax.random.normal(rng, dims, jnp.float32) * deviation
    if len(cuts) > 0:
        values = shard_levels(rng, dims, cuts, -0.22, 0.18) * values
    return jnp.clip(values, min=-most, max=most).astype(kind)


def setup_inputs(seed: int = 0) -> dict:
    streams_of = jax.random.split(jax.random.key(seed), 12)
    return {
        "terminal": scatter_about(streams_of[0], (WET_SLOT_TOTAL, BLOCK_CELLS, BLOCK_CELLS), 1.0, 6.0, ((0, 32),), jnp.float32),
        "depth": jnp.clip(jnp.exp(math.log(4.5) - 1.0986123 * jax.random.uniform(streams_of[1], (WET_SLOT_TOTAL, BLOCK_CELLS, BLOCK_CELLS), jnp.float32) ** shard_levels(streams_of[1], (WET_SLOT_TOTAL, BLOCK_CELLS, BLOCK_CELLS), ((0, 32),), -0.2, 0.2)), 1.5, 4.5),
        "wet_cells": draw_wet_cells(jax.random.fold_in(streams_of[11], 71), 0),
        "neighbours": draw_neighbours(jax.random.fold_in(streams_of[11], 71), 0),
        "gauge_cell": with_ends(jax.random.randint(streams_of[4], (DEVICES * G,), 0, BPD * BLOCK_CELLS * BLOCK_CELLS), jax.random.fold_in(streams_of[4], 1), 0, (BPD * BLOCK_CELLS * BLOCK_CELLS) - 1).astype(jnp.int32),
        "misfit": scatter_about(streams_of[5], (STEPS, DEVICES * G), 1.0, 6.0, ((1, 32),), jnp.float32),
        "basis": scatter_about(streams_of[6], (WET_SLOT_TOTAL, PATTERNS_PER_SLOT, BLOCK_CELLS, BLOCK_CELLS), (BLOCK_CELLS * BLOCK_CELLS) ** -0.5, 0.046875, ((0, 32),), jnp.float32),
        "subfault_index": draw_subfault_index(jax.random.fold_in(streams_of[11], 71), 0),
        "source": scatter_about(streams_of[8], (SUBFAULT_TOTAL,), 1.0, 6.0, ((0, 32),), jnp.float32),
        "background": scatter_about(streams_of[9], (SUBFAULT_TOTAL,), 1.0, 6.0, ((0, 32),), jnp.float32),
        "step_size": jnp.clip(jax.random.uniform(streams_of[10], (1,), jnp.float32, 0.25, 1.0), 0.25, 1.0),
    }


coupling = 0.5
prior_weight = 0.5


def fetch_edges(edges, nearby):
    present = nearby >= 0
    safe_index = jnp.where(present, nearby, 0).astype(jnp.int32)
    return jnp.where(present[:, None], edges[safe_index], jnp.zeros((), edges.dtype))


def along_x(field, west, east):
    ahead = jnp.concatenate([field[:, :, 1:], east[:, :, None]], axis=2)
    behind = jnp.concatenate([west[:, :, None], field[:, :, :-1]], axis=2)
    return 0.5 * (ahead - behind)


def along_y(field, south, north):
    ahead = jnp.concatenate([field[:, 1:, :], north[:, None, :]], axis=1)
    behind = jnp.concatenate([south[:, None, :], field[:, :-1, :]], axis=1)
    return 0.5 * (ahead - behind)


def reference(terminal, depth, wet_cells, neighbours, gauge_cell, misfit, basis, subfault_index, source, background, step_size):
    wet_float = wet_cells.astype(terminal.dtype)
    devices = N_BASIN * N_BLK
    per_device = BPD * BLOCK_CELLS * BLOCK_CELLS
    owners = (jnp.arange(devices * G) // G).astype(jnp.int32)
    flat_gauge = (owners * per_device + gauge_cell).astype(jnp.int32)
    surface = terminal
    east_flow = jnp.zeros_like(terminal)
    north_flow = jnp.zeros_like(terminal)
    for moment in range(STEPS):
        forcing = surface.reshape(-1).at[flat_gauge].add(misfit[moment]).reshape(surface.shape)
        masked = wet_float * forcing
        west_rim = fetch_edges(masked[:, :, -1], neighbours[:, 0])
        east_rim = fetch_edges(masked[:, :, 0], neighbours[:, 1])
        south_rim = fetch_edges(masked[:, -1, :], neighbours[:, 2])
        north_rim = fetch_edges(masked[:, 0, :], neighbours[:, 3])
        east_flow = wet_float * (east_flow + coupling * depth * along_x(masked, west_rim, east_rim))
        north_flow = wet_float * (north_flow + coupling * depth * along_y(masked, south_rim, north_rim))
        west_rim = fetch_edges(east_flow[:, :, -1], neighbours[:, 0])
        east_rim = fetch_edges(east_flow[:, :, 0], neighbours[:, 1])
        south_rim = fetch_edges(north_flow[:, -1, :], neighbours[:, 2])
        north_rim = fetch_edges(north_flow[:, 0, :], neighbours[:, 3])
        surface = masked + coupling * (along_x(east_flow, west_rim, east_rim) + along_y(north_flow, south_rim, north_rim))
    partial_value = jnp.einsum("sjyx,syx->sj", basis, surface, precision=lax.Precision.HIGHEST)
    projected = jax.ops.segment_sum(partial_value.reshape(-1), subfault_index.reshape(-1).astype(jnp.int32), num_segments=SUBFAULT_TOTAL)
    gradient = prior_weight * (source - background) + projected
    updated = source - step_size[0] * gradient
    return surface, updated
```

```python
import functools

import jax
import jax.numpy as jnp
from jax import lax
from jax.experimental import pallas as pl
from jax.experimental.pallas import tpu as pltpu
from jax.sharding import PartitionSpec as P

coupling = 0.5
prior_weight = 0.5
MESH = pl.DeviceIdType.MESH
PAD = 8
PAIR = 2


def kernel(
    basins,
    groups,
    owned,
    near_ref,
    subfault_ref,
    gauge_ref,
    misfit_ref,
    terminal_ref,
    depth_ref,
    wet_ref,
    basis_ref,
    surface_ref,
    mine_ref,
    terminal,
    depth,
    wet,
    basis,
    wet_f,
    across,
    along,
    across_md,
    along_md,
    across_flow,
    along_flow,
    edges,
    sums_out,
    sums_in,
    chosen,
    load_sem,
    send_sem,
    recv_sem,
    sums_sem,
    *halo_buffers,
):
    slots, side, _ = terminal.shape
    steps = misfit_ref.shape[0]
    outs, landings = halo_buffers[:steps], halo_buffers[steps:]
    patterns = basis.shape[1]
    entries = slots * 4
    devices = basins * groups
    peers = 3 * groups
    basin = lax.axis_index("basin")
    group = lax.axis_index("blk")
    me = basin * groups + group
    own_place = groups + group

    loads = [
        pltpu.make_async_copy(terminal_ref, terminal, load_sem.at[0]),
        pltpu.make_async_copy(wet_ref, wet, load_sem.at[1]),
        pltpu.make_async_copy(depth_ref, depth, load_sem.at[2]),
        pltpu.make_async_copy(basis_ref, basis, load_sem.at[3]),
    ]
    for load in loads:
        load.start()

    barrier = pltpu.get_barrier_semaphore()

    @pl.loop(1, devices)
    def _(k):
        other = (me + k) % devices
        pl.semaphore_signal(
            barrier, inc=1, device_id=(other // groups, other % groups), device_id_type=MESH
        )

    spare = peers * PAIR
    named = [near_ref[e // 4, e % 4] for e in range(entries)]
    there = [n >= 0 for n in named]
    safe = [jnp.maximum(n, 0) for n in named]
    holder = [n // slots for n in safe]
    source = [safe[e] % slots * 4 + (e % 4) + 1 - 2 * (e % 2) for e in range(entries)]
    local = [h == me for h in holder]
    heading = [(h // groups - basin + 1 + basins) % basins for h in holder]
    place = [
        jnp.where(there[e], heading[e] * groups + holder[e] % groups, -1) for e in range(entries)
    ]
    lookup = []
    for e in range(entries):
        rank = 0
        for f in range(entries):
            if f != e:
                earlier = (place[f] == place[e]) & (source[f] < source[e])
                rank = jnp.where(earlier, 1, rank)
        index = jnp.where(local[e], spare + source[e], place[e] * PAIR + rank)
        lookup.append(jnp.where(there[e], index, spare + entries))

    @pl.loop(0, peers)
    def _(p):
        low = entries
        high = entries
        for e in range(entries):
            high = jnp.where(place[e] == p, e, high)
        for e in reversed(range(entries)):
            low = jnp.where(place[e] == p, e, low)
        chosen[p * PAIR] = low
        chosen[p * PAIR + 1] = high

    gauge = gauge_ref[...].reshape(1, -1)
    count = gauge.shape[1]
    row_hot = jnp.where(
        lax.broadcasted_iota(jnp.int32, (slots * side, count), 0) == gauge // side, 1.0, 0.0
    )
    column_hot = lax.broadcasted_iota(jnp.int32, (side, count), 0) == gauge % side

    def injected(t):
        weights = jnp.where(column_hot, misfit_ref[t : t + 1, :], 0.0)
        return lax.dot_general(
            row_hot,
            weights,
            (((1,), (1,)), ((), ())),
            precision=lax.Precision.HIGHEST,
            preferred_element_type=jnp.float32,
        ).reshape(slots, side, side)

    for ref in (across_flow, along_flow):
        ref[...] = jnp.zeros_like(ref)
    edges[...] = jnp.zeros_like(edges)

    inside = slice(PAD, PAD + side)
    for load in loads[:3]:
        load.wait()
    for s in range(slots):
        m = wet[s].astype(jnp.float32)
        wet_f[s] = m
        md = m * depth[s] * (coupling * 0.5)
        along_md[s, inside] = md
        across_md[s, inside] = md.T

    def sends(t, out, landing):
        @pl.loop(1, peers)
        def _(k):
            p = (own_place + k) % peers
            p_heading = p // groups
            p_group = p % groups
            p_basin = (basin + p_heading - 1 + basins) % basins
            landing_at = (2 - p_heading) * groups + group
            pltpu.make_async_remote_copy(
                src_ref=out.at[pl.ds(p * PAIR, PAIR)],
                dst_ref=landing.at[pl.ds(landing_at * PAIR, PAIR)],
                send_sem=send_sem.at[t],
                recv_sem=recv_sem.at[t],
                device_id=(p_basin, p_group),
                device_id_type=MESH,
            ).start()

    def await_bytes(ref, sem):
        pltpu.make_async_copy(ref, ref, sem).wait()

    rest = slice(PAD - 1, PAD + side + 1)
    before = slice(PAD - 2, PAD + side)
    after = slice(PAD, PAD + side + 2)
    for t in range(steps):
        out, landing = outs[t], landings[t]
        force = injected(t)
        for s in range(slots):
            surface = terminal[s] if t == 0 else surface_ref[s]
            masked = wet_f[s] * (surface + force[s])
            along[s, inside] = masked
            across[s, inside] = masked.T
            for at, field, depths in ((0, across, across_md), (2, along, along_md)):
                edges[s * 4 + at, 0:2] = field[s, PAD : PAD + 2]
                edges[s * 4 + at + 1, 0:2] = field[s, PAD + side - 2 : PAD + side]
                if t == 0:
                    edges[s * 4 + at, 2:3] = depths[s, PAD : PAD + 1]
                    edges[s * 4 + at + 1, 2:3] = depths[s, PAD + side - 1 : PAD + side]
        width = 4 if t == 0 else 2
        for e in range(entries + 1):
            landing[spare + e] = edges[e, 0:width]
        for i in range(peers * PAIR):
            out[i] = edges[chosen[i], 0:width]
        if t == 0:
            pl.semaphore_wait(barrier, devices - 1)
        sends(t, out, landing)
        await_bytes(landing.at[pl.ds(0, (peers - 1) * PAIR)], recv_sem.at[t])
        for e in range(entries):
            s, at = e // 4, e % 4
            field, depths = (across, across_md) if at < 2 else (along, along_md)
            got = landing[lookup[e]]
            if at % 2 == 0:
                field[s, PAD - 2 : PAD] = got[0:2]
                if t == 0:
                    depths[s, PAD - 1 : PAD] = got[2:3]
            else:
                field[s, PAD + side : PAD + side + 2] = got[0:2]
                if t == 0:
                    depths[s, PAD + side : PAD + side + 1] = got[2:3]
        for s in range(slots):
            for field, depths, flow in (
                (across, across_md, across_flow),
                (along, along_md, along_flow),
            ):
                flow[s, rest] += depths[s, rest] * (field[s, after] - field[s, before])

            def gradient(flow):
                return (coupling * 0.5) * (
                    flow[s, PAD + 1 : PAD + side + 1] - flow[s, PAD - 1 : PAD + side - 1]
                )

            surface_ref[s] = along[s, inside] + (gradient(across_flow).T + gradient(along_flow))

    loads[3].wait()
    partial = []
    for s in range(slots):
        for j in range(patterns):
            down = jnp.sum(basis[s, j] * surface_ref[s], axis=0, keepdims=True)
            partial.append(jnp.sum(down, axis=1, keepdims=True))
    lanes = sums_out.shape[2]
    lane = lax.broadcasted_iota(jnp.int32, (1, lanes), 1)

    def share(device):
        row = jnp.zeros((1, lanes), jnp.float32)
        for e in range(slots * patterns):
            spot = subfault_ref[e // patterns, e % patterns] - device * owned
            row = row + jnp.where((lane == spot) & (lane < owned), partial[e], 0.0)
        return row

    @pl.loop(1, devices)
    def _(k):
        other = (me + k) % devices
        sums_out[other] = share(other)
        pltpu.make_async_remote_copy(
            src_ref=sums_out.at[other],
            dst_ref=sums_in.at[me],
            send_sem=sums_sem.at[0],
            recv_sem=sums_sem.at[1],
            device_id=(other // groups, other % groups),
            device_id_type=MESH,
        ).start()

    sums_in[me] = share(me)
    await_bytes(sums_in.at[pl.ds(0, devices - 1)], sums_sem.at[1])
    mine_ref[...] = jnp.sum(sums_in[...], axis=0)
    await_bytes(sums_out.at[pl.ds(0, devices - 1)], sums_sem.at[0])
    for t in range(steps):
        await_bytes(outs[t].at[pl.ds(0, (peers - 1) * PAIR)], send_sem.at[t])


def shards(
    terminal,
    depth,
    wet_cells,
    neighbours,
    gauge_cell,
    misfit,
    basis,
    subfault_index,
    source,
    background,
    step_size,
):
    slots, side, _ = terminal.shape
    steps = misfit.shape[0]
    owned = source.shape[0]
    basins = lax.axis_size("basin")
    groups = lax.axis_size("blk")
    devices = basins * groups
    rows = 3 * groups * PAIR
    entries = slots * 4
    kept = rows + entries + 1
    lanes = -(-owned // 128) * 128
    widths = [4] + [2] * (steps - 1)
    f32 = jnp.float32
    padded = pltpu.VMEM((slots, side + 2 * PAD, side), f32)
    smem = pl.BlockSpec(memory_space=pltpu.SMEM)
    vmem = pl.BlockSpec(memory_space=pltpu.VMEM)
    hbm = pl.BlockSpec(memory_space=pl.ANY)
    surface, mine = pl.pallas_call(
        functools.partial(kernel, basins, groups, owned),
        out_shape=(
            jax.ShapeDtypeStruct(terminal.shape, f32),
            jax.ShapeDtypeStruct((1, lanes), f32),
        ),
        in_specs=[smem, smem, vmem, vmem, hbm, hbm, hbm, hbm],
        out_specs=(vmem, vmem),
        scratch_shapes=[
            pltpu.VMEM(terminal.shape, f32),
            pltpu.VMEM(terminal.shape, f32),
            pltpu.VMEM(terminal.shape, jnp.int32),
            pltpu.VMEM(basis.shape, f32),
            pltpu.VMEM(terminal.shape, f32),
            padded,
            padded,
            padded,
            padded,
            padded,
            padded,
            pltpu.VMEM((entries + 1, 4, side), f32),
            pltpu.VMEM((devices, 1, lanes), f32),
            pltpu.VMEM((devices, 1, lanes), f32),
            pltpu.SMEM((rows,), jnp.int32),
            pltpu.SemaphoreType.DMA((4,)),
            pltpu.SemaphoreType.DMA((steps,)),
            pltpu.SemaphoreType.DMA((steps,)),
            pltpu.SemaphoreType.DMA((2,)),
            *[pltpu.VMEM((rows, width, side), f32) for width in widths],
            *[pltpu.VMEM((kept, width, side), f32) for width in widths],
        ],
        compiler_params=pltpu.CompilerParams(
            collective_id=0, has_side_effects=True, vmem_limit_bytes=32 * 1024 * 1024
        ),
        cost_estimate=pl.CostEstimate(flops=4_000_000, bytes_accessed=1_100_000, transcendentals=0),
        name="adjoint",
    )(neighbours, subfault_index, gauge_cell, misfit, terminal, depth, wet_cells, basis)
    gradient = prior_weight * (source - background) + mine[0, :owned]
    return (surface, source - step_size[0] * gradient)


def solution(mesh):
    in_specs = (
        P(("basin", "blk"), None, None),
        P(("basin", "blk"), None, None),
        P(("basin", "blk"), None, None),
        P(("basin", "blk"), None),
        P(("basin", "blk")),
        P(None, ("basin", "blk")),
        P(("basin", "blk"), None, None, None),
        P(("basin", "blk"), None),
        P(("basin", "blk")),
        P(("basin", "blk")),
        P(),
    )
    out_specs = (P(("basin", "blk"), None, None), P(("basin", "blk")))
    return jax.shard_map(shards, mesh=mesh, in_specs=in_specs, out_specs=out_specs, check_vma=False)
```

```python
import functools

import jax
import jax.numpy as jnp
from jax import lax
from jax.experimental import pallas as pl
from jax.experimental.pallas import tpu as pltpu
from jax.sharding import PartitionSpec as P

coupling = 0.5
prior_weight = 0.5
MESH = pl.DeviceIdType.MESH
PAD = 8
PAIR = 2


def wrapped(value, count):
    return jnp.where(value >= count, value - count, value)


def split_exact(x):
    high = x.astype(jnp.bfloat16)
    left = x - high.astype(jnp.float32)
    middle = left.astype(jnp.bfloat16)
    return high, middle, (left - middle.astype(jnp.float32)).astype(jnp.bfloat16)


def kernel(
    basins,
    groups,
    near_hbm,
    subfault_hbm,
    step_hbm,
    gauge_hbm,
    misfit_hbm,
    source_hbm,
    background_hbm,
    terminal_hbm,
    wet_hbm,
    depth_hbm,
    basis_hbm,
    surface_ref,
    updated_ref,
    near_ref,
    subfault_ref,
    step_ref,
    gauge_ref,
    misfit_ref,
    source_ref,
    background_ref,
    terminal,
    wet,
    depth,
    basis,
    wet_f,
    forces,
    across,
    along,
    across_md,
    along_md,
    across_flow,
    along_flow,
    edges,
    sums_out,
    sums_in,
    chosen,
    load_sem,
    send_sem,
    recv_sem,
    sums_sem,
    *halo_buffers,
):
    slots, side, _ = terminal.shape
    steps = misfit_ref.shape[0]
    outs, landings = halo_buffers[:steps], halo_buffers[steps:]
    patterns = basis.shape[1]
    owned = source_ref.shape[0]
    entries = slots * 4
    devices = basins * groups
    peers = 3 * groups
    basin = lax.axis_index("basin")
    group = lax.axis_index("blk")
    me = basin * groups + group

    pairs = (
        (near_hbm, near_ref),
        (subfault_hbm, subfault_ref),
        (step_hbm, step_ref),
        (gauge_hbm, gauge_ref),
        (misfit_hbm, misfit_ref),
        (source_hbm, source_ref),
        (background_hbm, background_ref),
        (terminal_hbm, terminal),
        (wet_hbm, wet),
        (depth_hbm, depth),
        (basis_hbm, basis),
    )
    loads = [pltpu.make_async_copy(a, b, load_sem.at[i]) for i, (a, b) in enumerate(pairs)]
    for load in loads:
        load.start()

    def each_peer(shifts, body):
        for shift in shifts:
            there = wrapped(basin + shift, basins)

            @pl.loop(1 if shift == 0 else 0, groups, unroll=min(groups, 8))
            def _(k):
                body(shift, there, wrapped(group + k, groups))

    barrier = pltpu.get_barrier_semaphore()

    def greet(shift, there, other):
        pl.semaphore_signal(barrier, inc=1, device_id=(there, other), device_id_type=MESH)

    each_peer(range(basins), greet)

    for ref in (across_flow, along_flow, edges):
        ref[...] = jnp.zeros_like(ref)

    loads[3].wait()
    loads[4].wait()
    gauge = gauge_ref[...].reshape(1, -1)
    count = gauge.shape[1]
    row_hot = lax.broadcasted_iota(jnp.int32, (slots * side, count), 0) == gauge // side
    row_hot = jnp.where(row_hot, 1.0, 0.0).astype(jnp.bfloat16)
    column_hot = lax.broadcasted_iota(jnp.int32, (side, count), 0) == gauge % side

    def injected(t):
        weights = jnp.where(column_hot, misfit_ref[t : t + 1, :], 0.0)
        total = None
        for part in split_exact(weights):
            term = lax.dot_general(
                row_hot, part, (((1,), (1,)), ((), ())), preferred_element_type=jnp.float32
            )
            total = term if total is None else total + term
        forces[...] = total.reshape(slots, side, side)

    injected(0)

    loads[0].wait()
    spare = peers * PAIR
    named = [near_ref[e // 4, e % 4] for e in range(entries)]
    present = [n >= 0 for n in named]
    safe = [jnp.maximum(n, 0) for n in named]
    holder = [n // slots for n in safe]
    origin = [safe[e] % slots * 4 + (e % 4) + 1 - 2 * (e % 2) for e in range(entries)]
    local = [h == me for h in holder]
    heading = [(h // groups - basin + 1 + basins) % basins for h in holder]
    place = [
        jnp.where(present[e], heading[e] * groups + holder[e] % groups, -1)
        for e in range(entries)
    ]
    lookup = []
    for e in range(entries):
        rank = 0
        for f in range(entries):
            if f != e:
                earlier = (place[f] == place[e]) & (origin[f] < origin[e])
                rank = jnp.where(earlier, 1, rank)
        index = jnp.where(local[e], spare + origin[e], place[e] * PAIR + rank)
        lookup.append(jnp.where(present[e], index, spare + entries))

    @pl.loop(0, peers, unroll=2)
    def _(p):
        low = entries
        high = entries
        for e in range(entries):
            high = jnp.where(place[e] == p, e, high)
        for e in reversed(range(entries)):
            low = jnp.where(place[e] == p, e, low)
        chosen[p * PAIR] = low
        chosen[p * PAIR + 1] = high

    inside = slice(PAD, PAD + side)
    for load in loads[7:10]:
        load.wait()
    for s in range(slots):
        m = wet[s].astype(jnp.float32)
        wet_f[s] = m
        md = m * depth[s] * (coupling * 0.5)
        along_md[s, inside] = md
        across_md[s, inside] = md.T

    def await_bytes(ref, sem):
        pltpu.make_async_copy(ref, ref, sem).wait()

    rest = slice(PAD - 1, PAD + side + 1)
    before = slice(PAD - 2, PAD + side)
    after = slice(PAD, PAD + side + 2)
    for t in range(steps):
        out, landing = outs[t], landings[t]
        for s in range(slots):
            surface = terminal[s] if t == 0 else surface_ref[s]
            masked = wet_f[s] * (surface + forces[s])
            along[s, inside] = masked
            across[s, inside] = masked.T
            for at, field, depths in ((0, across, across_md), (2, along, along_md)):
                edges[s * 4 + at, 0:2] = field[s, PAD : PAD + 2]
                edges[s * 4 + at + 1, 0:2] = field[s, PAD + side - 2 : PAD + side]
                if t == 0:
                    edges[s * 4 + at, 2:3] = depths[s, PAD : PAD + 1]
                    edges[s * 4 + at + 1, 2:3] = depths[s, PAD + side - 1 : PAD + side]
        width = 4 if t == 0 else 2
        for start in range(0, spare, 24):
            rows = range(start, min(start + 24, spare))
            picked = [edges[chosen[i], 0:width] for i in rows]
            for i, row in zip(rows, picked):
                out[i] = row
        if t == 0:
            pl.semaphore_wait(barrier, devices - 1)

        def send(shift, there, other):
            at = (0 if shift == basins - 1 else shift + 1) * groups
            landing_at = (2 * groups - at + group) * PAIR
            pltpu.make_async_remote_copy(
                src_ref=out.at[pl.ds((at + other) * PAIR, PAIR)],
                dst_ref=landing.at[pl.ds(landing_at, PAIR)],
                send_sem=send_sem.at[t],
                recv_sem=recv_sem.at[t],
                device_id=(there, other),
                device_id_type=MESH,
            ).start()

        each_peer((1, basins - 1, 0), send)
        for e in range(entries + 1):
            landing[spare + e] = edges[e, 0:width]
        if t + 1 < steps:
            injected(t + 1)
        await_bytes(landing.at[pl.ds(0, (peers - 1) * PAIR)], recv_sem.at[t])
        fetched = [landing[lookup[e]] for e in range(entries)]
        for e in range(entries):
            s, at = e // 4, e % 4
            field, depths = (across, across_md) if at < 2 else (along, along_md)
            got = fetched[e]
            if at % 2 == 0:
                field[s, PAD - 2 : PAD] = got[0:2]
                if t == 0:
                    depths[s, PAD - 1 : PAD] = got[2:3]
            else:
                field[s, PAD + side : PAD + side + 2] = got[0:2]
                if t == 0:
                    depths[s, PAD + side : PAD + side + 1] = got[2:3]
        for s in range(slots):
            for field, depths, flow in (
                (across, across_md, across_flow),
                (along, along_md, along_flow),
            ):
                flow[s, rest] += depths[s, rest] * (field[s, after] - field[s, before])

            def gradient(flow):
                return (coupling * 0.5) * (
                    flow[s, PAD + 1 : PAD + side + 1] - flow[s, PAD - 1 : PAD + side - 1]
                )

            surface_ref[s] = along[s, inside] + (gradient(across_flow).T + gradient(along_flow))

    for load in (loads[1], loads[2], loads[5], loads[6], loads[10]):
        load.wait()
    lanes = sums_out.shape[2]
    row = lax.broadcasted_iota(jnp.int32, (devices, lanes), 0)
    lane = lax.broadcasted_iota(jnp.int32, (devices, lanes), 1)
    number = jnp.where(lane < owned, row * owned + lane, -1)
    shares = jnp.zeros((devices, lanes), jnp.float32)
    for s in range(slots):
        for j in range(patterns):
            down = jnp.sum(basis[s, j] * surface_ref[s], axis=0, keepdims=True)
            partial = jnp.sum(down, axis=1, keepdims=True)
            shares = shares + jnp.where(number == subfault_ref[s, j], partial, 0.0)
    sums_out[...] = shares.reshape(devices, 1, lanes)

    def send_sum(shift, there, other):
        target = there * groups + other
        pltpu.make_async_remote_copy(
            src_ref=sums_out.at[target],
            dst_ref=sums_in.at[me],
            send_sem=sums_sem.at[0],
            recv_sem=sums_sem.at[1],
            device_id=(there, other),
            device_id_type=MESH,
        ).start()

    each_peer([*range(1, basins), 0], send_sum)
    sums_in[me] = sums_out[me]
    source = source_ref[...].reshape(1, owned)
    background = background_ref[...].reshape(1, owned)
    prior = prior_weight * (source - background)
    await_bytes(sums_in.at[pl.ds(0, devices - 1)], sums_sem.at[1])
    mine = jnp.sum(sums_in[...], axis=0)[:, :owned]
    updated_ref[...] = (source - step_ref[0] * (prior + mine)).reshape(owned)
    await_bytes(sums_out.at[pl.ds(0, devices - 1)], sums_sem.at[0])
    for t in range(steps):
        await_bytes(outs[t].at[pl.ds(0, (peers - 1) * PAIR)], send_sem.at[t])


def shards(
    terminal,
    depth,
    wet_cells,
    neighbours,
    gauge_cell,
    misfit,
    basis,
    subfault_index,
    source,
    background,
    step_size,
):
    slots, side, _ = terminal.shape
    steps = misfit.shape[0]
    owned = source.shape[0]
    basins = lax.axis_size("basin")
    groups = lax.axis_size("blk")
    devices = basins * groups
    rows = 3 * groups * PAIR
    entries = slots * 4
    kept = rows + entries + 1
    lanes = -(-owned // 128) * 128
    widths = [4] + [2] * (steps - 1)
    f32 = jnp.float32
    padded = pltpu.VMEM((slots, side + 2 * PAD, side), f32)
    vmem = pl.BlockSpec(memory_space=pltpu.VMEM)
    hbm = pl.BlockSpec(memory_space=pltpu.HBM)
    scalars = (neighbours, subfault_index, step_size)
    vectors = (
        gauge_cell,
        misfit,
        source,
        background,
        terminal,
        wet_cells,
        depth,
        basis,
    )
    operands = scalars + vectors
    return pl.pallas_call(
        functools.partial(kernel, basins, groups),
        out_shape=(
            jax.ShapeDtypeStruct(terminal.shape, f32),
            jax.ShapeDtypeStruct(source.shape, f32),
        ),
        in_specs=[hbm] * len(operands),
        out_specs=(vmem, vmem),
        scratch_shapes=[
            *[pltpu.SMEM(x.shape, x.dtype) for x in scalars],
            *[pltpu.VMEM(x.shape, x.dtype) for x in vectors],
            pltpu.VMEM(terminal.shape, f32),
            pltpu.VMEM(terminal.shape, f32),
            padded,
            padded,
            padded,
            padded,
            padded,
            padded,
            pltpu.VMEM((entries + 1, 4, side), f32),
            pltpu.VMEM((devices, 1, lanes), f32),
            pltpu.VMEM((devices, 1, lanes), f32),
            pltpu.SMEM((rows,), jnp.int32),
            pltpu.SemaphoreType.DMA((len(operands),)),
            pltpu.SemaphoreType.DMA((steps,)),
            pltpu.SemaphoreType.DMA((steps,)),
            pltpu.SemaphoreType.DMA((2,)),
            *[pltpu.VMEM((rows, width, side), f32) for width in widths],
            *[pltpu.VMEM((kept, width, side), f32) for width in widths],
        ],
        compiler_params=pltpu.CompilerParams(
            collective_id=0, has_side_effects=True, vmem_limit_bytes=32 * 1024 * 1024
        ),
        cost_estimate=pl.CostEstimate(flops=4_000_000, bytes_accessed=1_100_000, transcendentals=0),
        name="adjoint",
    )(*operands)


def solution(mesh):
    in_specs = (
        P(("basin", "blk"), None, None),
        P(("basin", "blk"), None, None),
        P(("basin", "blk"), None, None),
        P(("basin", "blk"), None),
        P(("basin", "blk")),
        P(None, ("basin", "blk")),
        P(("basin", "blk"), None, None, None),
        P(("basin", "blk"), None),
        P(("basin", "blk")),
        P(("basin", "blk")),
        P(),
    )
    out_specs = (P(("basin", "blk"), None, None), P(("basin", "blk")))
    return jax.shard_map(shards, mesh=mesh, in_specs=in_specs, out_specs=out_specs, check_vma=False)
```

```python
import functools

import jax
import jax.numpy as jnp
from jax import lax
from jax.experimental import pallas as pl
from jax.experimental.pallas import tpu as pltpu
from jax.sharding import PartitionSpec as P

coupling = 0.5
prior_weight = 0.5
MESH = pl.DeviceIdType.MESH
PAD = 8
PAIR = 2


def wrapped(value, count):
    return jnp.where(value >= count, value - count, value)


def split_exact(x):
    high = x.astype(jnp.bfloat16)
    left = x - high.astype(jnp.float32)
    middle = left.astype(jnp.bfloat16)
    return high, middle, (left - middle.astype(jnp.float32)).astype(jnp.bfloat16)


def kernel(
    basins,
    groups,
    near_hbm,
    subfault_hbm,
    step_hbm,
    gauge_hbm,
    misfit_hbm,
    source_hbm,
    background_hbm,
    terminal_hbm,
    wet_hbm,
    depth_hbm,
    basis_hbm,
    surface_hbm,
    updated_ref,
    near_ref,
    subfault_ref,
    step_ref,
    gauge_ref,
    misfit_ref,
    source_ref,
    background_ref,
    terminal,
    wet,
    depth,
    basis,
    surface_ref,
    wet_f,
    forces,
    across,
    along,
    across_md,
    along_md,
    across_flow,
    along_flow,
    edges,
    sums_out,
    sums_in,
    chosen,
    load_sem,
    send_sem,
    recv_sem,
    sums_sem,
    *halo_buffers,
):
    slots, side, _ = terminal.shape
    steps = misfit_ref.shape[0]
    outs, landings = halo_buffers[:steps], halo_buffers[steps:]
    patterns = basis.shape[1]
    owned = source_ref.shape[0]
    entries = slots * 4
    devices = basins * groups
    peers = 3 * groups
    basin = lax.axis_index("basin")
    group = lax.axis_index("blk")
    me = basin * groups + group

    pairs = (
        (near_hbm, near_ref),
        (subfault_hbm, subfault_ref),
        (step_hbm, step_ref),
        (gauge_hbm, gauge_ref),
        (misfit_hbm, misfit_ref),
        (source_hbm, source_ref),
        (background_hbm, background_ref),
        (terminal_hbm, terminal),
        (wet_hbm, wet),
        (depth_hbm, depth),
        (basis_hbm, basis),
    )
    loads = [pltpu.make_async_copy(a, b, load_sem.at[i]) for i, (a, b) in enumerate(pairs)]
    for load in loads:
        load.start()

    def each_peer(shifts, body):
        for shift in shifts:
            there = wrapped(basin + shift, basins)

            @pl.loop(1 if shift == 0 else 0, groups, unroll=min(groups, 8))
            def _(k):
                body(shift, there, wrapped(group + k, groups))

    barrier = pltpu.get_barrier_semaphore()

    def greet(shift, there, other):
        pl.semaphore_signal(barrier, inc=1, device_id=(there, other), device_id_type=MESH)

    each_peer(range(basins), greet)

    for ref in (across_flow, along_flow, edges):
        ref[...] = jnp.zeros_like(ref)

    loads[3].wait()
    loads[4].wait()
    gauge = gauge_ref[...].reshape(1, -1)
    count = gauge.shape[1]
    row_hot = lax.broadcasted_iota(jnp.int32, (slots * side, count), 0) == gauge // side
    row_hot = jnp.where(row_hot, 1.0, 0.0).astype(jnp.bfloat16)
    column_hot = lax.broadcasted_iota(jnp.int32, (side, count), 0) == gauge % side

    def injected(t):
        weights = jnp.where(column_hot, misfit_ref[t : t + 1, :], 0.0)
        total = None
        for part in split_exact(weights):
            term = lax.dot_general(
                row_hot, part, (((1,), (1,)), ((), ())), preferred_element_type=jnp.float32
            )
            total = term if total is None else total + term
        forces[...] = total.reshape(slots, side, side)

    injected(0)

    loads[0].wait()
    spare = peers * PAIR
    named = [near_ref[e // 4, e % 4] for e in range(entries)]
    present = [n >= 0 for n in named]
    safe = [jnp.maximum(n, 0) for n in named]
    holder = [n // slots for n in safe]
    origin = [safe[e] % slots * 4 + (e % 4) + 1 - 2 * (e % 2) for e in range(entries)]
    local = [h == me for h in holder]
    heading = [(h // groups - basin + 1 + basins) % basins for h in holder]
    place = [
        jnp.where(present[e], heading[e] * groups + holder[e] % groups, -1)
        for e in range(entries)
    ]
    lookup = []
    for e in range(entries):
        rank = 0
        for f in range(entries):
            if f != e:
                earlier = (place[f] == place[e]) & (origin[f] < origin[e])
                rank = jnp.where(earlier, 1, rank)
        index = jnp.where(local[e], spare + origin[e], place[e] * PAIR + rank)
        lookup.append(jnp.where(present[e], index, spare + entries))

    @pl.loop(0, peers, unroll=2)
    def _(p):
        low = entries
        high = entries
        for e in range(entries):
            high = jnp.where(place[e] == p, e, high)
        for e in reversed(range(entries)):
            low = jnp.where(place[e] == p, e, low)
        chosen[p * PAIR] = low
        chosen[p * PAIR + 1] = high

    inside = slice(PAD, PAD + side)
    for load in loads[7:10]:
        load.wait()
    for s in range(slots):
        m = wet[s].astype(jnp.float32)
        wet_f[s] = m
        md = m * depth[s] * (coupling * 0.5)
        along_md[s, inside] = md
        across_md[s, inside] = md.T

    def await_bytes(ref, sem):
        pltpu.make_async_copy(ref, ref, sem).wait()

    rest = slice(PAD - 1, PAD + side + 1)
    before = slice(PAD - 2, PAD + side)
    after = slice(PAD, PAD + side + 2)
    for t in range(steps):
        out, landing = outs[t], landings[t]
        for s in range(slots):
            surface = terminal[s] if t == 0 else surface_ref[s]
            masked = wet_f[s] * (surface + forces[s])
            along[s, inside] = masked
            across[s, inside] = masked.T
            for at, field, depths in ((0, across, across_md), (2, along, along_md)):
                edges[s * 4 + at, 0:2] = field[s, PAD : PAD + 2]
                edges[s * 4 + at + 1, 0:2] = field[s, PAD + side - 2 : PAD + side]
                if t == 0:
                    edges[s * 4 + at, 2:3] = depths[s, PAD : PAD + 1]
                    edges[s * 4 + at + 1, 2:3] = depths[s, PAD + side - 1 : PAD + side]
        width = 4 if t == 0 else 2
        for start in range(0, spare, 24):
            rows = range(start, min(start + 24, spare))
            picked = [edges[chosen[i], 0:width] for i in rows]
            for i, row in zip(rows, picked):
                out[i] = row
        if t == 0:
            pl.semaphore_wait(barrier, devices - 1)

        def send(shift, there, other):
            at = (0 if shift == basins - 1 else shift + 1) * groups
            landing_at = (2 * groups - at + group) * PAIR
            pltpu.make_async_remote_copy(
                src_ref=out.at[pl.ds((at + other) * PAIR, PAIR)],
                dst_ref=landing.at[pl.ds(landing_at, PAIR)],
                send_sem=send_sem.at[t],
                recv_sem=recv_sem.at[t],
                device_id=(there, other),
                device_id_type=MESH,
            ).start()

        each_peer((1, basins - 1, 0), send)
        for e in range(entries + 1):
            landing[spare + e] = edges[e, 0:width]
        if t + 1 < steps:
            injected(t + 1)
        await_bytes(landing.at[pl.ds(0, (peers - 1) * PAIR)], recv_sem.at[t])
        fetched = [landing[lookup[e]] for e in range(entries)]
        for e in range(entries):
            s, at = e // 4, e % 4
            field, depths = (across, across_md) if at < 2 else (along, along_md)
            got = fetched[e]
            if at % 2 == 0:
                field[s, PAD - 2 : PAD] = got[0:2]
                if t == 0:
                    depths[s, PAD - 1 : PAD] = got[2:3]
            else:
                field[s, PAD + side : PAD + side + 2] = got[0:2]
                if t == 0:
                    depths[s, PAD + side : PAD + side + 1] = got[2:3]
        for s in range(slots):
            for field, depths, flow in (
                (across, across_md, across_flow),
                (along, along_md, along_flow),
            ):
                flow[s, rest] += depths[s, rest] * (field[s, after] - field[s, before])

            def gradient(flow):
                return (coupling * 0.5) * (
                    flow[s, PAD + 1 : PAD + side + 1] - flow[s, PAD - 1 : PAD + side - 1]
                )

            surface_ref[s] = along[s, inside] + (gradient(across_flow).T + gradient(along_flow))

    store = pltpu.make_async_copy(surface_ref, surface_hbm, load_sem.at[len(pairs)])
    store.start()
    for load in (loads[1], loads[2], loads[5], loads[6], loads[10]):
        load.wait()
    lanes = sums_out.shape[2]
    row = lax.broadcasted_iota(jnp.int32, (devices, lanes), 0)
    lane = lax.broadcasted_iota(jnp.int32, (devices, lanes), 1)
    number = jnp.where(lane < owned, row * owned + lane, -1)
    shares = jnp.zeros((devices, lanes), jnp.float32)
    for s in range(slots):
        for j in range(patterns):
            down = jnp.sum(basis[s, j] * surface_ref[s], axis=0, keepdims=True)
            partial = jnp.sum(down, axis=1, keepdims=True)
            shares = shares + jnp.where(number == subfault_ref[s, j], partial, 0.0)
    sums_out[...] = shares.reshape(devices, 1, lanes)

    def send_sum(shift, there, other):
        target = there * groups + other
        pltpu.make_async_remote_copy(
            src_ref=sums_out.at[target],
            dst_ref=sums_in.at[me],
            send_sem=sums_sem.at[0],
            recv_sem=sums_sem.at[1],
            device_id=(there, other),
            device_id_type=MESH,
        ).start()

    each_peer([*range(1, basins), 0], send_sum)
    sums_in[me] = sums_out[me]
    source = source_ref[...].reshape(1, owned)
    background = background_ref[...].reshape(1, owned)
    prior = prior_weight * (source - background)
    await_bytes(sums_in.at[pl.ds(0, devices - 1)], sums_sem.at[1])
    mine = jnp.sum(sums_in[...], axis=0)[:, :owned]
    updated_ref[...] = (source - step_ref[0] * (prior + mine)).reshape(owned)
    store.wait()
    await_bytes(sums_out.at[pl.ds(0, devices - 1)], sums_sem.at[0])
    for t in range(steps):
        await_bytes(outs[t].at[pl.ds(0, (peers - 1) * PAIR)], send_sem.at[t])


def shards(
    terminal,
    depth,
    wet_cells,
    neighbours,
    gauge_cell,
    misfit,
    basis,
    subfault_index,
    source,
    background,
    step_size,
):
    slots, side, _ = terminal.shape
    steps = misfit.shape[0]
    owned = source.shape[0]
    basins = lax.axis_size("basin")
    groups = lax.axis_size("blk")
    devices = basins * groups
    rows = 3 * groups * PAIR
    entries = slots * 4
    kept = rows + entries + 1
    lanes = -(-owned // 128) * 128
    widths = [4] + [2] * (steps - 1)
    f32 = jnp.float32
    padded = pltpu.VMEM((slots, side + 2 * PAD, side), f32)
    vmem = pl.BlockSpec(memory_space=pltpu.VMEM)
    hbm = pl.BlockSpec(memory_space=pltpu.HBM)
    scalars = (neighbours, subfault_index, step_size)
    vectors = (
        gauge_cell,
        misfit,
        source,
        background,
        terminal,
        wet_cells,
        depth,
        basis,
    )
    operands = scalars + vectors
    return pl.pallas_call(
        functools.partial(kernel, basins, groups),
        out_shape=(
            jax.ShapeDtypeStruct(terminal.shape, f32),
            jax.ShapeDtypeStruct(source.shape, f32),
        ),
        in_specs=[hbm] * len(operands),
        out_specs=(hbm, vmem),
        scratch_shapes=[
            *[pltpu.SMEM(x.shape, x.dtype) for x in scalars],
            *[pltpu.VMEM(x.shape, x.dtype) for x in vectors],
            pltpu.VMEM(terminal.shape, f32),
            pltpu.VMEM(terminal.shape, f32),
            pltpu.VMEM(terminal.shape, f32),
            padded,
            padded,
            padded,
            padded,
            padded,
            padded,
            pltpu.VMEM((entries + 1, 4, side), f32),
            pltpu.VMEM((devices, 1, lanes), f32),
            pltpu.VMEM((devices, 1, lanes), f32),
            pltpu.SMEM((rows,), jnp.int32),
            pltpu.SemaphoreType.DMA((len(operands) + 1,)),
            pltpu.SemaphoreType.DMA((steps,)),
            pltpu.SemaphoreType.DMA((steps,)),
            pltpu.SemaphoreType.DMA((2,)),
            *[pltpu.VMEM((rows, width, side), f32) for width in widths],
            *[pltpu.VMEM((kept, width, side), f32) for width in widths],
        ],
        compiler_params=pltpu.CompilerParams(
            collective_id=0, has_side_effects=True, vmem_limit_bytes=64 * 1024 * 1024
        ),
        cost_estimate=pl.CostEstimate(flops=4_000_000, bytes_accessed=1_100_000, transcendentals=0),
        name="adjoint",
    )(*operands)


def solution(mesh):
    in_specs = (
        P(("basin", "blk"), None, None),
        P(("basin", "blk"), None, None),
        P(("basin", "blk"), None, None),
        P(("basin", "blk"), None),
        P(("basin", "blk")),
        P(None, ("basin", "blk")),
        P(("basin", "blk"), None, None, None),
        P(("basin", "blk"), None),
        P(("basin", "blk")),
        P(("basin", "blk")),
        P(),
    )
    out_specs = (P(("basin", "blk"), None, None), P(("basin", "blk")))
    return jax.shard_map(shards, mesh=mesh, in_specs=in_specs, out_specs=out_specs, check_vma=False)
```

```python
import functools

import jax
import jax.numpy as jnp
from jax import lax
from jax.experimental import pallas as pl
from jax.experimental.pallas import tpu as pltpu
from jax.sharding import PartitionSpec as P

coupling = 0.5
prior_weight = 0.5
MESH = pl.DeviceIdType.MESH
PAD = 8
PAIR = 2


def wrapped(value, count):
    return jnp.where(value >= count, value - count, value)


def split_exact(x):
    high = x.astype(jnp.bfloat16)
    left = x - high.astype(jnp.float32)
    middle = left.astype(jnp.bfloat16)
    return high, middle, (left - middle.astype(jnp.float32)).astype(jnp.bfloat16)


def kernel(
    basins,
    groups,
    near_hbm,
    subfault_hbm,
    step_hbm,
    gauge_hbm,
    misfit_hbm,
    source_hbm,
    background_hbm,
    terminal_hbm,
    wet_hbm,
    depth_hbm,
    basis_hbm,
    surface_hbm,
    updated_ref,
    near_ref,
    subfault_ref,
    step_ref,
    gauge_ref,
    misfit_ref,
    source_ref,
    background_ref,
    terminal,
    wet,
    depth,
    basis,
    surface_ref,
    wet_f,
    wet_t,
    forces,
    early_across,
    early_along,
    late_across,
    late_along,
    turned_across,
    turned_along,
    across,
    along,
    across_md,
    along_md,
    across_flow,
    along_flow,
    edges,
    weights,
    weights_out,
    weights_in,
    sums_out,
    sums_in,
    chosen,
    load_sem,
    send_sem,
    recv_sem,
    sums_sem,
    *halo_buffers,
):
    slots, side, _ = terminal.shape
    steps = misfit_ref.shape[0]
    outs, landings = halo_buffers[:steps], halo_buffers[steps:]
    patterns = basis.shape[1]
    owned = source_ref.shape[0]
    entries = slots * 4
    devices = basins * groups
    peers = 3 * groups
    basin = lax.axis_index("basin")
    group = lax.axis_index("blk")
    me = basin * groups + group

    pairs = (
        (near_hbm, near_ref),
        (subfault_hbm, subfault_ref),
        (step_hbm, step_ref),
        (gauge_hbm, gauge_ref),
        (misfit_hbm, misfit_ref),
        (source_hbm, source_ref),
        (background_hbm, background_ref),
        (terminal_hbm, terminal),
        (wet_hbm, wet),
        (depth_hbm, depth),
        (basis_hbm, basis),
    )
    loads = [pltpu.make_async_copy(a, b, load_sem.at[i]) for i, (a, b) in enumerate(pairs)]
    for load in loads:
        load.start()

    def each_peer(shifts, body):
        for shift in shifts:
            there = wrapped(basin + shift, basins)

            @pl.loop(1 if shift == 0 else 0, groups, unroll=min(groups, 8))
            def _(k):
                body(shift, there, wrapped(group + k, groups))

    barrier = pltpu.get_barrier_semaphore()

    def greet(shift, there, other):
        pl.semaphore_signal(barrier, inc=1, device_id=(there, other), device_id_type=MESH)

    each_peer(range(basins), greet)

    zeroed = (across, along, across_md, along_md, across_flow, along_flow, late_across, late_along)
    for ref in (*zeroed, edges, weights):
        ref[...] = jnp.zeros_like(ref)

    loads[3].wait()
    loads[4].wait()
    gauge = gauge_ref[...].reshape(1, -1)
    count = gauge.shape[1]
    row_hot = lax.broadcasted_iota(jnp.int32, (slots * side, count), 0) == gauge // side
    row_hot = jnp.where(row_hot, 1.0, 0.0).astype(jnp.bfloat16)
    column_hot = lax.broadcasted_iota(jnp.int32, (side, count), 0) == gauge % side

    def injected(t):
        weights = jnp.where(column_hot, misfit_ref[t : t + 1, :], 0.0)
        total = None
        for part in split_exact(weights):
            term = lax.dot_general(
                row_hot, part, (((1,), (1,)), ((), ())), preferred_element_type=jnp.float32
            )
            total = term if total is None else total + term
        forces[...] = total.reshape(slots, side, side)

    injected(0)

    loads[0].wait()
    spare = peers * PAIR
    named = [near_ref[e // 4, e % 4] for e in range(entries)]
    present = [n >= 0 for n in named]
    safe = [jnp.maximum(n, 0) for n in named]
    holder = [n // slots for n in safe]
    origin = [safe[e] % slots * 4 + (e % 4) + 1 - 2 * (e % 2) for e in range(entries)]
    local = [h == me for h in holder]
    heading = [(h // groups - basin + 1 + basins) % basins for h in holder]
    place = [
        jnp.where(present[e], heading[e] * groups + holder[e] % groups, -1)
        for e in range(entries)
    ]
    lookup = []
    for e in range(entries):
        rank = 0
        for f in range(entries):
            if f != e:
                earlier = (place[f] == place[e]) & (origin[f] < origin[e])
                rank = jnp.where(earlier, 1, rank)
        index = jnp.where(local[e], spare + origin[e], place[e] * PAIR + rank)
        lookup.append(jnp.where(present[e], index, spare + entries))

    @pl.loop(0, peers, unroll=2)
    def _(p):
        low = entries
        high = entries
        for e in range(entries):
            high = jnp.where(place[e] == p, e, high)
        for e in reversed(range(entries)):
            low = jnp.where(place[e] == p, e, low)
        chosen[p * PAIR] = low
        chosen[p * PAIR + 1] = high

    inside = slice(PAD, PAD + side)
    for load in loads[7:10]:
        load.wait()
    def await_bytes(ref, sem):
        pltpu.make_async_copy(ref, ref, sem).wait()

    for s in range(slots):
        m = wet[s].astype(jnp.float32)
        wet_f[s] = m
        wet_t[s] = m.T
        md = m * depth[s] * (coupling * 0.5)
        along_md[s, inside] = md
        across_md[s, inside] = md.T
        masked = m * (terminal[s] + forces[s])
        along[s, inside] = masked
        across[s, inside] = masked.T

    ways = (
        (across, across_md, across_flow, wet_t, early_across, late_across, turned_along),
        (along, along_md, along_flow, wet_f, early_along, late_along, turned_across),
    )
    first, last = PAD, PAD + side - 1
    half = coupling * 0.5
    lane_row = lax.broadcasted_iota(jnp.int32, (1, side), 1)
    for load in (loads[1], loads[10]):
        load.wait()
    for s in range(slots):
        names = jnp.zeros((1, side), jnp.float32)
        for j in range(patterns):
            names = jnp.where(lane_row == j, subfault_ref[s, j].astype(jnp.float32), names)
        for w, (_, depths, *_) in enumerate(ways):
            low = s * 4 + 2 * w
            edges[low, 2:3] = depths[s, first : first + 1]
            edges[low + 1, 2:3] = depths[s, last : last + 1]
            for e in (low, low + 1):
                edges[e, 3:4] = names

    def pick(table, out, rows):
        for start in range(0, spare, 24):
            span = range(start, min(start + 24, spare))
            picked = [table[chosen[i], 0:rows] for i in span]
            for i, row in zip(span, picked):
                out[i] = row

    def keep_own(table, landing, rows):
        for e in range(entries + 1):
            landing[spare + e] = table[e, 0:rows]

    def send_all(out, landing, at_sem):
        def send(shift, there, other):
            at = (0 if shift == basins - 1 else shift + 1) * groups
            landing_at = (2 * groups - at + group) * PAIR
            pltpu.make_async_remote_copy(
                src_ref=out.at[pl.ds((at + other) * PAIR, PAIR)],
                dst_ref=landing.at[pl.ds(landing_at, PAIR)],
                send_sem=send_sem.at[at_sem],
                recv_sem=recv_sem.at[at_sem],
                device_id=(there, other),
                device_id_type=MESH,
            ).start()

        each_peer((1, basins - 1, 0), send)

    def send_weights():
        for s in range(slots):
            for j in range(patterns):
                upright = basis[s, j]
                for w, (field, turned) in enumerate(((across_md, upright.T), (along_md, upright))):
                    low = s * 4 + 2 * w
                    for e, outer, inner, md_at in (
                        (low, 0, 1, first),
                        (low + 1, side - 1, side - 2, last),
                    ):
                        near = half * turned[inner : inner + 1] * field[s, md_at : md_at + 1]
                        weights[e, 2 * j : 2 * j + 1] = near
                        weights[e, 2 * j + 1 : 2 * j + 2] = half * turned[outer : outer + 1]
        pick(weights, weights_out, 2 * patterns)
        send_all(weights_out, weights_in, steps)
        keep_own(weights, weights_in, 2 * patterns)

    def partial_sums(facing):
        await_bytes(weights_in.at[pl.ds(0, (peers - 1) * PAIR)], recv_sem.at[steps])
        lanes = sums_out.shape[2]
        row = lax.broadcasted_iota(jnp.int32, (devices, lanes), 0)
        lane = lax.broadcasted_iota(jnp.int32, (devices, lanes), 1)
        number = jnp.where(lane < owned, row * owned + lane, -1)
        number_f = number.astype(jnp.float32)
        shares = jnp.zeros((devices, lanes), jnp.float32)
        for s in range(slots):
            for j in range(patterns):
                down = jnp.sum(basis[s, j] * surface_ref[s], axis=0, keepdims=True)
                partial = jnp.sum(down, axis=1, keepdims=True)
                shares = shares + jnp.where(number == subfault_ref[s, j], partial, 0.0)
        odd = lax.broadcasted_iota(jnp.int32, (2 * patterns, side), 0) % 2 == 1
        for e in range(entries):
            near, far = (0, 1) if e % 2 == 0 else (1, 0)
            near_row = edges[e, near : near + 1]
            far_row = edges[e, far : far + 1] * edges[e, 2:3]
            terms = weights_in[lookup[e]] * jnp.where(odd, far_row, near_row)
            dots = jnp.sum(terms, axis=1, keepdims=True)
            for j in range(patterns):
                dot = dots[2 * j : 2 * j + 1] + dots[2 * j + 1 : 2 * j + 2]
                shares = shares + jnp.where(number_f == facing[e][:, j : j + 1], dot, 0.0)
        sums_out[...] = shares.reshape(devices, 1, lanes)

    def send_sums():
        def send_sum(shift, there, other):
            target = there * groups + other
            pltpu.make_async_remote_copy(
                src_ref=sums_out.at[target],
                dst_ref=sums_in.at[me],
                send_sem=sums_sem.at[0],
                recv_sem=sums_sem.at[1],
                device_id=(there, other),
                device_id_type=MESH,
            ).start()

        each_peer([*range(1, basins), 0], send_sum)
        sums_in[me] = sums_out[me]

    rest = slice(PAD - 1, PAD + side + 1)
    before = slice(PAD - 2, PAD + side)
    after = slice(PAD, PAD + side + 2)
    facing = None
    for t in range(steps):
        out, landing = outs[t], landings[t]
        for s in range(slots):
            for w, (field, _, _, mask, early, late, turned) in enumerate(ways):
                for e, at in ((s * 4 + 2 * w, 0), (s * 4 + 2 * w + 1, side - 2)):
                    if t == 0:
                        edges[e, 0:2] = field[s, PAD + at : PAD + at + 2]
                    else:
                        two = slice(at, at + 2)
                        edges[e, 0:2] = early[s, two] + mask[s, two] * (
                            late[s, two] + turned[s, two]
                        )
        rows = 4 if t == 0 else 2
        pick(edges, out, rows)
        if t == 0:
            pl.semaphore_wait(barrier, devices - 1)
        send_all(out, landing, t)

        keep_own(edges, landing, rows)
        if t == 0:
            send_weights()
        if t + 1 < steps:
            injected(t + 1)
        for s in range(slots):
            for field, depths, flow, mask, early, late, turned in ways:
                if t > 0:
                    field[s, inside] = early[s] + mask[s] * (late[s] + turned[s])
                flow[s, rest] += depths[s, rest] * (field[s, after] - field[s, before])

            def gradient(flow):
                return half * (
                    flow[s, PAD + 1 : PAD + side + 1] - flow[s, PAD - 1 : PAD + side - 1]
                )

            surface = along[s, inside] + (gradient(across_flow).T + gradient(along_flow))
            if t + 1 < steps:
                masked = wet_f[s] * (surface + forces[s])
                early_along[s] = masked
                early_across[s] = masked.T
            else:
                surface_ref[s] = surface
        if t + 1 == steps:
            partial_sums(facing)
            send_sums()

        await_bytes(landing.at[pl.ds(0, (peers - 1) * PAIR)], recv_sem.at[t])
        fetched = [landing[lookup[e]] for e in range(entries)]
        if t == 0:
            facing = [got[3:4] for got in fetched]
        for s in range(slots):
            for w, (field, depths, flow, mask, early, late, turned) in enumerate(ways):
                low, high = fetched[s * 4 + 2 * w], fetched[s * 4 + 2 * w + 1]
                far_low, far_high = -low[0:1], high[1:2]
                if t == 0:
                    depths[s, first - 1 : first] = low[2:3]
                    depths[s, last + 1 : last + 2] = high[2:3]
                    far_low = field[s, first : first + 1] + far_low
                    far_high = far_high - field[s, last : last + 1]
                far_low = depths[s, first - 1 : first] * far_low
                near_low = -depths[s, first : first + 1] * low[1:2]
                near_high = depths[s, last : last + 1] * high[0:1]
                far_high = depths[s, last + 1 : last + 2] * far_high
                late[s, 0:1] = -half * far_low
                late[s, 1:2] = -half * near_low
                late[s, side - 2 : side - 1] = half * near_high
                late[s, side - 1 : side] = half * far_high
                if t + 1 < steps:
                    flow[s, first - 1 : first] += far_low
                    flow[s, first : first + 1] += near_low
                    flow[s, last : last + 1] += near_high
                    flow[s, last + 1 : last + 2] += far_high
        for s in range(slots):
            turned_across[s] = late_across[s].T
            if t + 1 < steps:
                turned_along[s] = late_along[s].T
            else:
                surface_ref[s] += late_along[s] + turned_across[s]

    store = pltpu.make_async_copy(surface_ref, surface_hbm, load_sem.at[len(pairs)])
    store.start()
    for load in (loads[2], loads[5], loads[6]):
        load.wait()
    source = source_ref[...].reshape(1, owned)
    background = background_ref[...].reshape(1, owned)
    prior = prior_weight * (source - background)
    await_bytes(sums_in.at[pl.ds(0, devices - 1)], sums_sem.at[1])
    mine = jnp.sum(sums_in[...], axis=0)[:, :owned]
    updated_ref[...] = (source - step_ref[0] * (prior + mine)).reshape(owned)
    store.wait()
    await_bytes(sums_out.at[pl.ds(0, devices - 1)], sums_sem.at[0])
    for t in range(steps):
        await_bytes(outs[t].at[pl.ds(0, (peers - 1) * PAIR)], send_sem.at[t])
    await_bytes(weights_out.at[pl.ds(0, (peers - 1) * PAIR)], send_sem.at[steps])


def shards(
    terminal,
    depth,
    wet_cells,
    neighbours,
    gauge_cell,
    misfit,
    basis,
    subfault_index,
    source,
    background,
    step_size,
):
    slots, side, _ = terminal.shape
    steps = misfit.shape[0]
    patterns = basis.shape[1]
    owned = source.shape[0]
    basins = lax.axis_size("basin")
    groups = lax.axis_size("blk")
    devices = basins * groups
    rows = 3 * groups * PAIR
    entries = slots * 4
    kept = rows + entries + 1
    lanes = -(-owned // 128) * 128
    widths = [4] + [2] * (steps - 1)
    f32 = jnp.float32
    padded = pltpu.VMEM((slots, side + 2 * PAD, side), f32)
    vmem = pl.BlockSpec(memory_space=pltpu.VMEM)
    hbm = pl.BlockSpec(memory_space=pltpu.HBM)
    scalars = (neighbours, subfault_index, step_size)
    vectors = (
        gauge_cell,
        misfit,
        source,
        background,
        terminal,
        wet_cells,
        depth,
        basis,
    )
    operands = scalars + vectors
    return pl.pallas_call(
        functools.partial(kernel, basins, groups),
        out_shape=(
            jax.ShapeDtypeStruct(terminal.shape, f32),
            jax.ShapeDtypeStruct(source.shape, f32),
        ),
        in_specs=[hbm] * len(operands),
        out_specs=(hbm, vmem),
        scratch_shapes=[
            *[pltpu.SMEM(x.shape, x.dtype) for x in scalars],
            *[pltpu.VMEM(x.shape, x.dtype) for x in vectors],
            *[pltpu.VMEM(terminal.shape, f32)] * 10,
            padded,
            padded,
            padded,
            padded,
            padded,
            padded,
            pltpu.VMEM((entries + 1, 4, side), f32),
            pltpu.VMEM((entries + 1, 2 * patterns, side), f32),
            pltpu.VMEM((rows, 2 * patterns, side), f32),
            pltpu.VMEM((kept, 2 * patterns, side), f32),
            pltpu.VMEM((devices, 1, lanes), f32),
            pltpu.VMEM((devices, 1, lanes), f32),
            pltpu.SMEM((rows,), jnp.int32),
            pltpu.SemaphoreType.DMA((len(operands) + 1,)),
            pltpu.SemaphoreType.DMA((steps + 1,)),
            pltpu.SemaphoreType.DMA((steps + 1,)),
            pltpu.SemaphoreType.DMA((2,)),
            *[pltpu.VMEM((rows, width, side), f32) for width in widths],
            *[pltpu.VMEM((kept, width, side), f32) for width in widths],
        ],
        compiler_params=pltpu.CompilerParams(
            collective_id=0, has_side_effects=True, vmem_limit_bytes=64 * 1024 * 1024
        ),
        cost_estimate=pl.CostEstimate(flops=4_000_000, bytes_accessed=1_100_000, transcendentals=0),
        name="adjoint",
    )(*operands)


def solution(mesh):
    in_specs = (
        P(("basin", "blk"), None, None),
        P(("basin", "blk"), None, None),
        P(("basin", "blk"), None, None),
        P(("basin", "blk"), None),
        P(("basin", "blk")),
        P(None, ("basin", "blk")),
        P(("basin", "blk"), None, None, None),
        P(("basin", "blk"), None),
        P(("basin", "blk")),
        P(("basin", "blk")),
        P(),
    )
    out_specs = (P(("basin", "blk"), None, None), P(("basin", "blk")))
    return jax.shard_map(shards, mesh=mesh, in_specs=in_specs, out_specs=out_specs, check_vma=False)
```

```python
import functools

import jax
import jax.numpy as jnp
from jax import lax
from jax.experimental import pallas as pl
from jax.experimental.pallas import tpu as pltpu
from jax.sharding import PartitionSpec as P

coupling = 0.5
prior_weight = 0.5
MESH = pl.DeviceIdType.MESH
PAD = 8
PAIR = 2


def wrapped(value, count):
    return jnp.where(value >= count, value - count, value)


def split_exact(x):
    high = x.astype(jnp.bfloat16)
    left = x - high.astype(jnp.float32)
    middle = left.astype(jnp.bfloat16)
    return high, middle, (left - middle.astype(jnp.float32)).astype(jnp.bfloat16)


def weight_plan(steps, patterns):
    first = min(1, steps - 2)
    chunks = min(steps - 1 - first, patterns)
    return first, chunks, -(-patterns // chunks)


def kernel(
    basins,
    groups,
    near_hbm,
    subfault_hbm,
    step_hbm,
    gauge_hbm,
    misfit_hbm,
    source_hbm,
    background_hbm,
    terminal_hbm,
    wet_hbm,
    depth_hbm,
    basis_hbm,
    surface_hbm,
    updated_ref,
    near_ref,
    subfault_ref,
    step_ref,
    gauge_ref,
    misfit_ref,
    source_ref,
    background_ref,
    terminal,
    wet,
    depth,
    basis,
    surface_ref,
    wet_f,
    wet_t,
    forces,
    early_across,
    early_along,
    late_across,
    late_along,
    turned_across,
    turned_along,
    across,
    along,
    across_md,
    along_md,
    across_flow,
    along_flow,
    edges,
    weights,
    sums_out,
    sums_in,
    chosen,
    load_sem,
    send_sem,
    recv_sem,
    sums_sem,
    *halo_buffers,
):
    slots, side, _ = terminal.shape
    steps = misfit_ref.shape[0]
    patterns = basis.shape[1]
    first_chunk, chunks, per_chunk = weight_plan(steps, patterns)
    outs, landings = halo_buffers[:steps], halo_buffers[steps : 2 * steps]
    weights_out = halo_buffers[2 * steps : 2 * steps + chunks]
    weights_in = halo_buffers[2 * steps + chunks :]
    owned = source_ref.shape[0]
    entries = slots * 4
    devices = basins * groups
    peers = 3 * groups
    basin = lax.axis_index("basin")
    group = lax.axis_index("blk")
    me = basin * groups + group

    pairs = (
        (near_hbm, near_ref),
        (subfault_hbm, subfault_ref),
        (step_hbm, step_ref),
        (gauge_hbm, gauge_ref),
        (misfit_hbm, misfit_ref),
        (source_hbm, source_ref),
        (background_hbm, background_ref),
        (terminal_hbm, terminal),
        (wet_hbm, wet),
        (depth_hbm, depth),
        (basis_hbm, basis),
    )
    loads = [pltpu.make_async_copy(a, b, load_sem.at[i]) for i, (a, b) in enumerate(pairs)]
    for load in loads:
        load.start()

    def each_peer(shifts, body):
        for shift in shifts:
            there = wrapped(basin + shift, basins)

            @pl.loop(1 if shift == 0 else 0, groups, unroll=min(groups, 8))
            def _(k):
                body(shift, there, wrapped(group + k, groups))

    barrier = pltpu.get_barrier_semaphore()

    def greet(shift, there, other):
        pl.semaphore_signal(barrier, inc=1, device_id=(there, other), device_id_type=MESH)

    each_peer(range(basins), greet)

    zeroed = (across, along, across_md, along_md, across_flow, along_flow, late_across, late_along)
    for ref in (*zeroed, edges, weights):
        ref[...] = jnp.zeros_like(ref)

    loads[3].wait()
    loads[4].wait()
    gauge = gauge_ref[...].reshape(1, -1)
    count = gauge.shape[1]
    row_hot = lax.broadcasted_iota(jnp.int32, (slots * side, count), 0) == gauge // side
    row_hot = jnp.where(row_hot, 1.0, 0.0).astype(jnp.bfloat16)
    column_hot = lax.broadcasted_iota(jnp.int32, (side, count), 0) == gauge % side

    def injected(t):
        weights = jnp.where(column_hot, misfit_ref[t : t + 1, :], 0.0)
        total = None
        for part in split_exact(weights):
            term = lax.dot_general(
                row_hot, part, (((1,), (1,)), ((), ())), preferred_element_type=jnp.float32
            )
            total = term if total is None else total + term
        forces[...] = total.reshape(slots, side, side)

    injected(0)

    loads[0].wait()
    spare = peers * PAIR
    named = [near_ref[e // 4, e % 4] for e in range(entries)]
    present = [n >= 0 for n in named]
    safe = [jnp.maximum(n, 0) for n in named]
    holder = [n // slots for n in safe]
    origin = [safe[e] % slots * 4 + (e % 4) + 1 - 2 * (e % 2) for e in range(entries)]
    local = [h == me for h in holder]
    heading = [(h // groups - basin + 1 + basins) % basins for h in holder]
    place = [
        jnp.where(present[e], heading[e] * groups + holder[e] % groups, -1)
        for e in range(entries)
    ]
    lookup = []
    for e in range(entries):
        rank = 0
        for f in range(entries):
            if f != e:
                earlier = (place[f] == place[e]) & (origin[f] < origin[e])
                rank = jnp.where(earlier, 1, rank)
        index = jnp.where(local[e], spare + origin[e], place[e] * PAIR + rank)
        lookup.append(jnp.where(present[e], index, spare + entries))

    @pl.loop(0, peers, unroll=2)
    def _(p):
        low = entries
        high = entries
        for e in range(entries):
            high = jnp.where(place[e] == p, e, high)
        for e in reversed(range(entries)):
            low = jnp.where(place[e] == p, e, low)
        chosen[p * PAIR] = low
        chosen[p * PAIR + 1] = high

    inside = slice(PAD, PAD + side)
    for load in loads[7:10]:
        load.wait()
    def await_bytes(ref, sem):
        pltpu.make_async_copy(ref, ref, sem).wait()

    for s in range(slots):
        m = wet[s].astype(jnp.float32)
        wet_f[s] = m
        wet_t[s] = m.T
        md = m * depth[s] * (coupling * 0.5)
        along_md[s, inside] = md
        across_md[s, inside] = md.T
        masked = m * (terminal[s] + forces[s])
        along[s, inside] = masked
        across[s, inside] = masked.T

    ways = (
        (across, across_md, across_flow, wet_t, early_across, late_across, turned_along),
        (along, along_md, along_flow, wet_f, early_along, late_along, turned_across),
    )
    first, last = PAD, PAD + side - 1
    half = coupling * 0.5
    lane_row = lax.broadcasted_iota(jnp.int32, (1, side), 1)
    for load in (loads[1], loads[10]):
        load.wait()
    for s in range(slots):
        names = jnp.zeros((1, side), jnp.float32)
        for j in range(patterns):
            names = jnp.where(lane_row == j, subfault_ref[s, j].astype(jnp.float32), names)
        for w, (_, depths, *_) in enumerate(ways):
            low = s * 4 + 2 * w
            edges[low, 2:3] = depths[s, first : first + 1]
            edges[low + 1, 2:3] = depths[s, last : last + 1]
            for e in (low, low + 1):
                edges[e, 3:4] = names

    def pick(table, out, rows):
        for start in range(0, spare, 24):
            span = range(start, min(start + 24, spare))
            picked = [table[chosen[i], 0:rows] for i in span]
            for i, row in zip(span, picked):
                out[i] = row

    def keep_own(table, landing, rows):
        for e in range(entries + 1):
            landing[spare + e] = table[e, 0:rows]

    def send_all(out, landing, at_sem):
        def send(shift, there, other):
            at = (0 if shift == basins - 1 else shift + 1) * groups
            landing_at = (2 * groups - at + group) * PAIR
            pltpu.make_async_remote_copy(
                src_ref=out.at[pl.ds((at + other) * PAIR, PAIR)],
                dst_ref=landing.at[pl.ds(landing_at, PAIR)],
                send_sem=send_sem.at[at_sem],
                recv_sem=recv_sem.at[at_sem],
                device_id=(there, other),
                device_id_type=MESH,
            ).start()

        each_peer((1, basins - 1, 0), send)

    def send_weights(c):
        own = range(c * per_chunk, min((c + 1) * per_chunk, patterns))
        for s in range(slots):
            for i, j in enumerate(own):
                upright = basis[s, j]
                for w, (field, turned) in enumerate(((across_md, upright.T), (along_md, upright))):
                    low = s * 4 + 2 * w
                    for e, outer, inner, md_at in (
                        (low, 0, 1, first),
                        (low + 1, side - 1, side - 2, last),
                    ):
                        near = half * turned[inner : inner + 1] * field[s, md_at : md_at + 1]
                        weights[c, e, 2 * i : 2 * i + 1] = near
                        weights[c, e, 2 * i + 1 : 2 * i + 2] = half * turned[outer : outer + 1]
        pick(weights.at[c], weights_out[c], 2 * per_chunk)
        send_all(weights_out[c], weights_in[c], steps + c)
        keep_own(weights.at[c], weights_in[c], 2 * per_chunk)

    def partial_sums(facing):
        for c in range(chunks):
            await_bytes(weights_in[c].at[pl.ds(0, (peers - 1) * PAIR)], recv_sem.at[steps + c])
        lanes = sums_out.shape[2]
        row = lax.broadcasted_iota(jnp.int32, (devices, lanes), 0)
        lane = lax.broadcasted_iota(jnp.int32, (devices, lanes), 1)
        number = jnp.where(lane < owned, row * owned + lane, -1)
        number_f = number.astype(jnp.float32)
        shares = jnp.zeros((devices, lanes), jnp.float32)
        for s in range(slots):
            for j in range(patterns):
                down = jnp.sum(basis[s, j] * surface_ref[s], axis=0, keepdims=True)
                partial = jnp.sum(down, axis=1, keepdims=True)
                shares = shares + jnp.where(number == subfault_ref[s, j], partial, 0.0)
        odd = lax.broadcasted_iota(jnp.int32, (2 * per_chunk, side), 0) % 2 == 1
        for e in range(entries):
            near, far = (0, 1) if e % 2 == 0 else (1, 0)
            near_row = edges[e, near : near + 1]
            far_row = edges[e, far : far + 1] * edges[e, 2:3]
            for c in range(chunks):
                terms = weights_in[c][lookup[e]] * jnp.where(odd, far_row, near_row)
                dots = jnp.sum(terms, axis=1, keepdims=True)
                for i, j in enumerate(range(c * per_chunk, min((c + 1) * per_chunk, patterns))):
                    dot = dots[2 * i : 2 * i + 1] + dots[2 * i + 1 : 2 * i + 2]
                    shares = shares + jnp.where(number_f == facing[e][:, j : j + 1], dot, 0.0)
        sums_out[...] = shares.reshape(devices, 1, lanes)

    def send_sums():
        def send_sum(shift, there, other):
            target = there * groups + other
            pltpu.make_async_remote_copy(
                src_ref=sums_out.at[target],
                dst_ref=sums_in.at[me],
                send_sem=sums_sem.at[0],
                recv_sem=sums_sem.at[1],
                device_id=(there, other),
                device_id_type=MESH,
            ).start()

        each_peer([*range(1, basins), 0], send_sum)
        sums_in[me] = sums_out[me]

    rest = slice(PAD - 1, PAD + side + 1)
    before = slice(PAD - 2, PAD + side)
    after = slice(PAD, PAD + side + 2)
    facing = None
    for t in range(steps):
        out, landing = outs[t], landings[t]
        for s in range(slots):
            for w, (field, _, _, mask, early, late, turned) in enumerate(ways):
                for e, at in ((s * 4 + 2 * w, 0), (s * 4 + 2 * w + 1, side - 2)):
                    if t == 0:
                        edges[e, 0:2] = field[s, PAD + at : PAD + at + 2]
                    else:
                        two = slice(at, at + 2)
                        edges[e, 0:2] = early[s, two] + mask[s, two] * (
                            late[s, two] + turned[s, two]
                        )
        rows = 4 if t == 0 else 2
        pick(edges, out, rows)
        if t == 0:
            pl.semaphore_wait(barrier, devices - 1)
        send_all(out, landing, t)

        keep_own(edges, landing, rows)
        if first_chunk <= t < first_chunk + chunks:
            send_weights(t - first_chunk)
        if t + 1 < steps:
            injected(t + 1)
        for s in range(slots):
            for field, depths, flow, mask, early, late, turned in ways:
                if t > 0:
                    field[s, inside] = early[s] + mask[s] * (late[s] + turned[s])
                flow[s, rest] += depths[s, rest] * (field[s, after] - field[s, before])

            def gradient(flow):
                return half * (
                    flow[s, PAD + 1 : PAD + side + 1] - flow[s, PAD - 1 : PAD + side - 1]
                )

            surface = along[s, inside] + (gradient(across_flow).T + gradient(along_flow))
            if t + 1 < steps:
                masked = wet_f[s] * (surface + forces[s])
                early_along[s] = masked
                early_across[s] = masked.T
            else:
                surface_ref[s] = surface
        if t + 1 == steps:
            partial_sums(facing)
            send_sums()

        await_bytes(landing.at[pl.ds(0, (peers - 1) * PAIR)], recv_sem.at[t])
        fetched = [landing[lookup[e]] for e in range(entries)]
        if t == 0:
            facing = [got[3:4] for got in fetched]
        for s in range(slots):
            for w, (field, depths, flow, mask, early, late, turned) in enumerate(ways):
                low, high = fetched[s * 4 + 2 * w], fetched[s * 4 + 2 * w + 1]
                far_low, far_high = -low[0:1], high[1:2]
                if t == 0:
                    depths[s, first - 1 : first] = low[2:3]
                    depths[s, last + 1 : last + 2] = high[2:3]
                    far_low = field[s, first : first + 1] + far_low
                    far_high = far_high - field[s, last : last + 1]
                far_low = depths[s, first - 1 : first] * far_low
                near_low = -depths[s, first : first + 1] * low[1:2]
                near_high = depths[s, last : last + 1] * high[0:1]
                far_high = depths[s, last + 1 : last + 2] * far_high
                late[s, 0:1] = -half * far_low
                late[s, 1:2] = -half * near_low
                late[s, side - 2 : side - 1] = half * near_high
                late[s, side - 1 : side] = half * far_high
                if t + 1 < steps:
                    flow[s, first - 1 : first] += far_low
                    flow[s, first : first + 1] += near_low
                    flow[s, last : last + 1] += near_high
                    flow[s, last + 1 : last + 2] += far_high
        for s in range(slots):
            turned_across[s] = late_across[s].T
            if t + 1 < steps:
                turned_along[s] = late_along[s].T
            else:
                surface_ref[s] += late_along[s] + turned_across[s]

    store = pltpu.make_async_copy(surface_ref, surface_hbm, load_sem.at[len(pairs)])
    store.start()
    for load in (loads[2], loads[5], loads[6]):
        load.wait()
    source = source_ref[...].reshape(1, owned)
    background = background_ref[...].reshape(1, owned)
    prior = prior_weight * (source - background)
    await_bytes(sums_in.at[pl.ds(0, devices - 1)], sums_sem.at[1])
    mine = jnp.sum(sums_in[...], axis=0)[:, :owned]
    updated_ref[...] = (source - step_ref[0] * (prior + mine)).reshape(owned)
    store.wait()
    await_bytes(sums_out.at[pl.ds(0, devices - 1)], sums_sem.at[0])
    for t in range(steps):
        await_bytes(outs[t].at[pl.ds(0, (peers - 1) * PAIR)], send_sem.at[t])
    for c in range(chunks):
        await_bytes(weights_out[c].at[pl.ds(0, (peers - 1) * PAIR)], send_sem.at[steps + c])


def hand_over(surface, updated, surface_out, updated_out, sem):
    first = pltpu.make_async_copy(surface, surface_out, sem.at[0])
    second = pltpu.make_async_copy(updated, updated_out, sem.at[1])
    first.start()
    second.start()
    first.wait()
    second.wait()


def shards(
    terminal,
    depth,
    wet_cells,
    neighbours,
    gauge_cell,
    misfit,
    basis,
    subfault_index,
    source,
    background,
    step_size,
):
    slots, side, _ = terminal.shape
    steps = misfit.shape[0]
    patterns = basis.shape[1]
    first_chunk, chunks, per_chunk = weight_plan(steps, patterns)
    owned = source.shape[0]
    basins = lax.axis_size("basin")
    groups = lax.axis_size("blk")
    devices = basins * groups
    rows = 3 * groups * PAIR
    entries = slots * 4
    kept = rows + entries + 1
    lanes = -(-owned // 128) * 128
    widths = [4] + [2] * (steps - 1)
    f32 = jnp.float32
    padded = pltpu.VMEM((slots, side + 2 * PAD, side), f32)
    vmem = pl.BlockSpec(memory_space=pltpu.VMEM)
    hbm = pl.BlockSpec(memory_space=pltpu.HBM)
    scalars = (neighbours, subfault_index, step_size)
    vectors = (
        gauge_cell,
        misfit,
        source,
        background,
        terminal,
        wet_cells,
        depth,
        basis,
    )
    operands = scalars + vectors
    results = pl.pallas_call(
        functools.partial(kernel, basins, groups),
        out_shape=(
            jax.ShapeDtypeStruct(terminal.shape, f32),
            jax.ShapeDtypeStruct(source.shape, f32),
        ),
        in_specs=[hbm] * len(operands),
        out_specs=(hbm, vmem),
        scratch_shapes=[
            *[pltpu.SMEM(x.shape, x.dtype) for x in scalars],
            *[pltpu.VMEM(x.shape, x.dtype) for x in vectors],
            *[pltpu.VMEM(terminal.shape, f32)] * 10,
            padded,
            padded,
            padded,
            padded,
            padded,
            padded,
            pltpu.VMEM((entries + 1, 4, side), f32),
            pltpu.VMEM((chunks, entries + 1, 2 * per_chunk, side), f32),
            pltpu.VMEM((devices, 1, lanes), f32),
            pltpu.VMEM((devices, 1, lanes), f32),
            pltpu.SMEM((rows,), jnp.int32),
            pltpu.SemaphoreType.DMA((len(operands) + 1,)),
            pltpu.SemaphoreType.DMA((steps + chunks,)),
            pltpu.SemaphoreType.DMA((steps + chunks,)),
            pltpu.SemaphoreType.DMA((2,)),
            *[pltpu.VMEM((rows, width, side), f32) for width in widths],
            *[pltpu.VMEM((kept, width, side), f32) for width in widths],
            *[pltpu.VMEM((rows, 2 * per_chunk, side), f32)] * chunks,
            *[pltpu.VMEM((kept, 2 * per_chunk, side), f32)] * chunks,
        ],
        compiler_params=pltpu.CompilerParams(
            collective_id=0, has_side_effects=True, vmem_limit_bytes=64 * 1024 * 1024
        ),
        cost_estimate=pl.CostEstimate(flops=4_000_000, bytes_accessed=1_100_000, transcendentals=0),
        name="adjoint",
    )(*operands)
    return pl.pallas_call(
        hand_over,
        out_shape=tuple(jax.ShapeDtypeStruct(x.shape, x.dtype) for x in results),
        in_specs=[hbm] * 2,
        out_specs=(hbm, hbm),
        scratch_shapes=[pltpu.SemaphoreType.DMA((2,))],
        compiler_params=pltpu.CompilerParams(vmem_limit_bytes=64 * 1024 * 1024),
        name="hand_over",
    )(*results)


def solution(mesh):
    in_specs = (
        P(("basin", "blk"), None, None),
        P(("basin", "blk"), None, None),
        P(("basin", "blk"), None, None),
        P(("basin", "blk"), None),
        P(("basin", "blk")),
        P(None, ("basin", "blk")),
        P(("basin", "blk"), None, None, None),
        P(("basin", "blk"), None),
        P(("basin", "blk")),
        P(("basin", "blk")),
        P(),
    )
    out_specs = (P(("basin", "blk"), None, None), P(("basin", "blk")))
    return jax.shard_map(shards, mesh=mesh, in_specs=in_specs, out_specs=out_specs, check_vma=False)
```

```python
import functools

import jax
import jax.numpy as jnp
from jax import lax
from jax.experimental import pallas as pl
from jax.experimental.pallas import tpu as pltpu
from jax.sharding import PartitionSpec as P

coupling = 0.5
prior_weight = 0.5
MESH = pl.DeviceIdType.MESH
PAD = 8
PIECES = 4
PAIR = 2


def wrapped(value, count):
    return jnp.where(value >= count, value - count, value)


def split_exact(x):
    high = x.astype(jnp.bfloat16)
    left = x - high.astype(jnp.float32)
    middle = left.astype(jnp.bfloat16)
    return high, middle, (left - middle.astype(jnp.float32)).astype(jnp.bfloat16)


def weight_plan(steps, patterns):
    first = 0
    chunks = 1
    return first, chunks, -(-patterns // chunks)


def kernel(
    basins,
    groups,
    near_hbm,
    subfault_hbm,
    step_hbm,
    gauge_hbm,
    misfit_hbm,
    source_hbm,
    background_hbm,
    terminal_hbm,
    wet_hbm,
    depth_hbm,
    basis_hbm,
    surface_hbm,
    updated_ref,
    near_ref,
    subfault_ref,
    step_ref,
    gauge_ref,
    misfit_ref,
    source_ref,
    background_ref,
    terminal,
    wet,
    depth,
    basis,
    surface_ref,
    wet_f,
    wet_t,
    forces,
    early_across,
    early_along,
    late_across,
    late_along,
    turned_across,
    turned_along,
    across,
    along,
    across_md,
    along_md,
    across_flow,
    along_flow,
    edges,
    weights,
    sums_out,
    sums_in,
    chosen,
    load_sem,
    send_sem,
    recv_sem,
    sums_sem,
    *halo_buffers,
):
    slots, side, _ = terminal.shape
    steps = misfit_ref.shape[0]
    patterns = basis.shape[1]
    first_chunk, chunks, per_chunk = weight_plan(steps, patterns)
    outs, landings = halo_buffers[:steps], halo_buffers[steps : 2 * steps]
    weights_out = halo_buffers[2 * steps : 2 * steps + chunks]
    weights_in = halo_buffers[2 * steps + chunks :]
    owned = source_ref.shape[0]
    entries = slots * 4
    devices = basins * groups
    peers = 3 * groups
    basin = lax.axis_index("basin")
    group = lax.axis_index("blk")
    me = basin * groups + group

    pairs = (
        (near_hbm, near_ref),
        (subfault_hbm, subfault_ref),
        (step_hbm, step_ref),
        (gauge_hbm, gauge_ref),
        (misfit_hbm, misfit_ref),
        (source_hbm, source_ref),
        (background_hbm, background_ref),
        (terminal_hbm, terminal),
        (wet_hbm, wet),
        (depth_hbm, depth),
        (basis_hbm, basis),
    )
    loads = [pltpu.make_async_copy(a, b, load_sem.at[i]) for i, (a, b) in enumerate(pairs)]
    for load in loads:
        load.start()

    def each_peer(shifts, body):
        for shift in shifts:
            there = wrapped(basin + shift, basins)

            @pl.loop(1 if shift == 0 else 0, groups, unroll=min(groups, 8))
            def _(k):
                body(shift, there, wrapped(group + k, groups))

    barrier = pltpu.get_barrier_semaphore()

    def greet(shift, there, other):
        pl.semaphore_signal(barrier, inc=1, device_id=(there, other), device_id_type=MESH)

    each_peer(range(basins), greet)

    zeroed = (across, along, across_md, along_md, across_flow, along_flow, late_across, late_along)
    for ref in (*zeroed, edges, weights):
        ref[...] = jnp.zeros_like(ref)

    loads[3].wait()
    loads[4].wait()
    gauge = gauge_ref[...].reshape(1, -1)
    count = gauge.shape[1]
    row_hot = lax.broadcasted_iota(jnp.int32, (slots * side, count), 0) == gauge // side
    row_hot = jnp.where(row_hot, 1.0, 0.0).astype(jnp.bfloat16)
    column_hot = lax.broadcasted_iota(jnp.int32, (side, count), 0) == gauge % side

    def injected(t):
        weights = jnp.where(column_hot, misfit_ref[t : t + 1, :], 0.0)
        total = None
        for part in split_exact(weights):
            term = lax.dot_general(
                row_hot, part, (((1,), (1,)), ((), ())), preferred_element_type=jnp.float32
            )
            total = term if total is None else total + term
        forces[...] = total.reshape(slots, side, side)

    injected(0)

    loads[0].wait()
    spare = peers * PAIR
    named = [near_ref[e // 4, e % 4] for e in range(entries)]
    present = [n >= 0 for n in named]
    safe = [jnp.maximum(n, 0) for n in named]
    holder = [n // slots for n in safe]
    origin = [safe[e] % slots * 4 + (e % 4) + 1 - 2 * (e % 2) for e in range(entries)]
    local = [h == me for h in holder]
    heading = [(h // groups - basin + 1 + basins) % basins for h in holder]
    place = [
        jnp.where(present[e], heading[e] * groups + holder[e] % groups, -1)
        for e in range(entries)
    ]
    lookup = []
    for e in range(entries):
        rank = 0
        for f in range(entries):
            if f != e:
                earlier = (place[f] == place[e]) & (origin[f] < origin[e])
                rank = jnp.where(earlier, 1, rank)
        index = jnp.where(local[e], spare + origin[e], place[e] * PAIR + rank)
        lookup.append(jnp.where(present[e], index, spare + entries))

    @pl.loop(0, peers, unroll=2)
    def _(p):
        low = entries
        high = entries
        for e in range(entries):
            high = jnp.where(place[e] == p, e, high)
        for e in reversed(range(entries)):
            low = jnp.where(place[e] == p, e, low)
        chosen[p * PAIR] = low
        chosen[p * PAIR + 1] = high

    inside = slice(PAD, PAD + side)
    for load in loads[7:10]:
        load.wait()
    def await_bytes(ref, sem):
        pltpu.make_async_copy(ref, ref, sem).wait()

    for s in range(slots):
        m = wet[s].astype(jnp.float32)
        wet_f[s] = m
        wet_t[s] = m.T
        md = m * depth[s] * (coupling * 0.5)
        along_md[s, inside] = md
        across_md[s, inside] = md.T
        masked = m * (terminal[s] + forces[s])
        along[s, inside] = masked
        across[s, inside] = masked.T

    ways = (
        (across, across_md, across_flow, wet_t, early_across, late_across, turned_along),
        (along, along_md, along_flow, wet_f, early_along, late_along, turned_across),
    )
    first, last = PAD, PAD + side - 1
    half = coupling * 0.5
    lane_row = lax.broadcasted_iota(jnp.int32, (1, side), 1)
    for load in (loads[1], loads[10]):
        load.wait()
    for s in range(slots):
        names = jnp.zeros((1, side), jnp.float32)
        for j in range(patterns):
            names = jnp.where(lane_row == j, subfault_ref[s, j].astype(jnp.float32), names)
        for w, (_, depths, *_) in enumerate(ways):
            low = s * 4 + 2 * w
            edges[low, 2:3] = depths[s, first : first + 1]
            edges[low + 1, 2:3] = depths[s, last : last + 1]
            for e in (low, low + 1):
                edges[e, 3:4] = names

    def pick(table, out, rows):
        for start in range(0, spare, 24):
            span = range(start, min(start + 24, spare))
            picked = [table[chosen[i], 0:rows] for i in span]
            for i, row in zip(span, picked):
                out[i] = row

    def keep_own(table, landing, rows):
        for e in range(entries + 1):
            landing[spare + e] = table[e, 0:rows]

    def send_all(out, landing, at_sem):
        def send(shift, there, other):
            at = (0 if shift == basins - 1 else shift + 1) * groups
            landing_at = (2 * groups - at + group) * PAIR
            pltpu.make_async_remote_copy(
                src_ref=out.at[pl.ds((at + other) * PAIR, PAIR)],
                dst_ref=landing.at[pl.ds(landing_at, PAIR)],
                send_sem=send_sem.at[at_sem],
                recv_sem=recv_sem.at[at_sem],
                device_id=(there, other),
                device_id_type=MESH,
            ).start()

        each_peer((1, basins - 1, 0), send)

    def send_weights(c):
        own = range(c * per_chunk, min((c + 1) * per_chunk, patterns))
        for s in range(slots):
            for i, j in enumerate(own):
                upright = basis[s, j]
                for w, (field, turned) in enumerate(((across_md, upright.T), (along_md, upright))):
                    low = s * 4 + 2 * w
                    for e, outer, inner, md_at in (
                        (low, 0, 1, first),
                        (low + 1, side - 1, side - 2, last),
                    ):
                        near = half * turned[inner : inner + 1] * field[s, md_at : md_at + 1]
                        weights[c, e, 2 * i : 2 * i + 1] = near
                        weights[c, e, 2 * i + 1 : 2 * i + 2] = half * turned[outer : outer + 1]
        pick(weights.at[c], weights_out[c], 2 * per_chunk)
        send_all(weights_out[c], weights_in[c], steps + c)
        keep_own(weights.at[c], weights_in[c], 2 * per_chunk)

    def partial_sums(facing):
        for c in range(chunks):
            await_bytes(weights_in[c].at[pl.ds(0, (peers - 1) * PAIR)], recv_sem.at[steps + c])
        lanes = sums_out.shape[2]
        row = lax.broadcasted_iota(jnp.int32, (devices, lanes), 0)
        lane = lax.broadcasted_iota(jnp.int32, (devices, lanes), 1)
        number = jnp.where(lane < owned, row * owned + lane, -1)
        number_f = number.astype(jnp.float32)
        shares = jnp.zeros((devices, lanes), jnp.float32)
        for s in range(slots):
            for j in range(patterns):
                down = jnp.sum(basis[s, j] * surface_ref[s], axis=0, keepdims=True)
                partial = jnp.sum(down, axis=1, keepdims=True)
                shares = shares + jnp.where(number == subfault_ref[s, j], partial, 0.0)
        odd = lax.broadcasted_iota(jnp.int32, (2 * per_chunk, side), 0) % 2 == 1
        for e in range(entries):
            near, far = (0, 1) if e % 2 == 0 else (1, 0)
            near_row = edges[e, near : near + 1]
            far_row = edges[e, far : far + 1] * edges[e, 2:3]
            for c in range(chunks):
                terms = weights_in[c][lookup[e]] * jnp.where(odd, far_row, near_row)
                dots = jnp.sum(terms, axis=1, keepdims=True)
                for i, j in enumerate(range(c * per_chunk, min((c + 1) * per_chunk, patterns))):
                    dot = dots[2 * i : 2 * i + 1] + dots[2 * i + 1 : 2 * i + 2]
                    shares = shares + jnp.where(number_f == facing[e][:, j : j + 1], dot, 0.0)
        sums_out[...] = shares.reshape(devices, 1, lanes)

    def send_sums():
        def send_sum(shift, there, other):
            target = there * groups + other
            pltpu.make_async_remote_copy(
                src_ref=sums_out.at[target],
                dst_ref=sums_in.at[me],
                send_sem=sums_sem.at[0],
                recv_sem=sums_sem.at[1],
                device_id=(there, other),
                device_id_type=MESH,
            ).start()

        each_peer([*range(1, basins), 0], send_sum)
        sums_in[me] = sums_out[me]

    rest = slice(PAD - 1, PAD + side + 1)
    before = slice(PAD - 2, PAD + side)
    after = slice(PAD, PAD + side + 2)
    facing = None
    outer_lanes = (0, 1, side - 2, side - 1)
    late_rows = {}
    for t in range(steps):
        out, landing = outs[t], landings[t]
        for s in range(slots):
            for w, (field, _, _, mask, early, late, turned) in enumerate(ways):
                for e, at in ((s * 4 + 2 * w, 0), (s * 4 + 2 * w + 1, side - 2)):
                    if t == 0:
                        edges[e, 0:2] = field[s, PAD + at : PAD + at + 2]
                    else:
                        for r in range(2):
                            y = at + r
                            own = late_rows[s, w][outer_lanes.index(y)]
                            crossing = jnp.zeros_like(own)
                            for x, other in zip(outer_lanes, late_rows[s, 1 - w]):
                                crossing = jnp.where(lane_row == x, other[:, y : y + 1], crossing)
                            edges[e, r : r + 1] = early[s, y : y + 1] + mask[s, y : y + 1] * (
                                own + crossing
                            )
        rows = 4 if t == 0 else 2
        pick(edges, out, rows)
        if t == 0:
            pl.semaphore_wait(barrier, devices - 1)
        send_all(out, landing, t)

        keep_own(edges, landing, rows)
        if first_chunk <= t < first_chunk + chunks:
            send_weights(t - first_chunk)
        if t + 1 < steps:
            injected(t + 1)
        for s in range(slots):
            if t > 0:
                turned_across[s] = late_across[s].T
                turned_along[s] = late_along[s].T
            for field, depths, flow, mask, early, late, turned in ways:
                if t > 0:
                    field[s, inside] = early[s] + mask[s] * (late[s] + turned[s])
                flow[s, rest] += depths[s, rest] * (field[s, after] - field[s, before])

            def gradient(flow):
                return half * (
                    flow[s, PAD + 1 : PAD + side + 1] - flow[s, PAD - 1 : PAD + side - 1]
                )

            surface = along[s, inside] + (gradient(across_flow).T + gradient(along_flow))
            if t + 1 < steps:
                masked = wet_f[s] * (surface + forces[s])
                early_along[s] = masked
                early_across[s] = masked.T
            else:
                surface_ref[s] = surface
        if t + 1 == steps:
            partial_sums(facing)
            send_sums()

        await_bytes(landing.at[pl.ds(0, (peers - 1) * PAIR)], recv_sem.at[t])
        fetched = [landing[lookup[e]] for e in range(entries)]
        if t == 0:
            facing = [got[3:4] for got in fetched]
        for s in range(slots):
            for w, (field, depths, flow, mask, early, late, turned) in enumerate(ways):
                low, high = fetched[s * 4 + 2 * w], fetched[s * 4 + 2 * w + 1]
                far_low, far_high = -low[0:1], high[1:2]
                if t == 0:
                    depths[s, first - 1 : first] = low[2:3]
                    depths[s, last + 1 : last + 2] = high[2:3]
                    far_low = field[s, first : first + 1] + far_low
                    far_high = far_high - field[s, last : last + 1]
                far_low = depths[s, first - 1 : first] * far_low
                near_low = -depths[s, first : first + 1] * low[1:2]
                near_high = depths[s, last : last + 1] * high[0:1]
                far_high = depths[s, last + 1 : last + 2] * far_high
                late_rows[s, w] = (
                    -half * far_low,
                    -half * near_low,
                    half * near_high,
                    half * far_high,
                )
                for y, late_row in zip(outer_lanes, late_rows[s, w]):
                    late[s, y : y + 1] = late_row
                if t + 1 < steps:
                    flow[s, first - 1 : first] += far_low
                    flow[s, first : first + 1] += near_low
                    flow[s, last : last + 1] += near_high
                    flow[s, last + 1 : last + 2] += far_high

    for s in range(slots):
        surface_ref[s] += late_along[s] + late_across[s].T
    store = pltpu.make_async_copy(surface_ref, surface_hbm, load_sem.at[len(pairs)])
    store.start()
    for load in (loads[2], loads[5], loads[6]):
        load.wait()
    source = source_ref[...].reshape(1, owned)
    background = background_ref[...].reshape(1, owned)
    prior = prior_weight * (source - background)
    await_bytes(sums_in.at[pl.ds(0, devices - 1)], sums_sem.at[1])
    mine = jnp.sum(sums_in[...], axis=0)[:, :owned]
    updated_ref[...] = (source - step_ref[0] * (prior + mine)).reshape(owned)
    store.wait()
    await_bytes(sums_out.at[pl.ds(0, devices - 1)], sums_sem.at[0])
    for t in range(steps):
        await_bytes(outs[t].at[pl.ds(0, (peers - 1) * PAIR)], send_sem.at[t])
    for c in range(chunks):
        await_bytes(weights_out[c].at[pl.ds(0, (peers - 1) * PAIR)], send_sem.at[steps + c])


def hand_over(surface, updated, surface_out, updated_out, surface_held, updated_held, sem):
    slots, side, _ = surface.shape
    size = side // PIECES
    moves = [(updated, updated_held, updated_out)]
    for s in range(slots):
        for i in range(PIECES):
            part = (s, pl.ds(i * size, size))
            moves.append((surface.at[part], surface_held.at[part], surface_out.at[part]))
    ins = [pltpu.make_async_copy(a, b, sem.at[0, i]) for i, (a, b, _) in enumerate(moves)]
    outs = [pltpu.make_async_copy(b, c, sem.at[1, i]) for i, (_, b, c) in enumerate(moves)]
    for copy in ins:
        copy.start()
    for arrived, copy in zip(ins, outs):
        arrived.wait()
        copy.start()
    for copy in outs:
        copy.wait()


def shards(
    terminal,
    depth,
    wet_cells,
    neighbours,
    gauge_cell,
    misfit,
    basis,
    subfault_index,
    source,
    background,
    step_size,
):
    slots, side, _ = terminal.shape
    steps = misfit.shape[0]
    patterns = basis.shape[1]
    first_chunk, chunks, per_chunk = weight_plan(steps, patterns)
    owned = source.shape[0]
    basins = lax.axis_size("basin")
    groups = lax.axis_size("blk")
    devices = basins * groups
    rows = 3 * groups * PAIR
    entries = slots * 4
    kept = rows + entries + 1
    lanes = -(-owned // 128) * 128
    widths = [4] + [2] * (steps - 1)
    f32 = jnp.float32
    padded = pltpu.VMEM((slots, side + 2 * PAD, side), f32)
    vmem = pl.BlockSpec(memory_space=pltpu.VMEM)
    hbm = pl.BlockSpec(memory_space=pltpu.HBM)
    scalars = (neighbours, subfault_index, step_size)
    vectors = (
        gauge_cell,
        misfit,
        source,
        background,
        terminal,
        wet_cells,
        depth,
        basis,
    )
    operands = scalars + vectors
    results = pl.pallas_call(
        functools.partial(kernel, basins, groups),
        out_shape=(
            jax.ShapeDtypeStruct(terminal.shape, f32),
            jax.ShapeDtypeStruct(source.shape, f32),
        ),
        in_specs=[hbm] * len(operands),
        out_specs=(hbm, vmem),
        scratch_shapes=[
            *[pltpu.SMEM(x.shape, x.dtype) for x in scalars],
            *[pltpu.VMEM(x.shape, x.dtype) for x in vectors],
            *[pltpu.VMEM(terminal.shape, f32)] * 10,
            padded,
            padded,
            padded,
            padded,
            padded,
            padded,
            pltpu.VMEM((entries + 1, 4, side), f32),
            pltpu.VMEM((chunks, entries + 1, 2 * per_chunk, side), f32),
            pltpu.VMEM((devices, 1, lanes), f32),
            pltpu.VMEM((devices, 1, lanes), f32),
            pltpu.SMEM((rows,), jnp.int32),
            pltpu.SemaphoreType.DMA((len(operands) + 1,)),
            pltpu.SemaphoreType.DMA((steps + chunks,)),
            pltpu.SemaphoreType.DMA((steps + chunks,)),
            pltpu.SemaphoreType.DMA((2,)),
            *[pltpu.VMEM((rows, width, side), f32) for width in widths],
            *[pltpu.VMEM((kept, width, side), f32) for width in widths],
            *[pltpu.VMEM((rows, 2 * per_chunk, side), f32)] * chunks,
            *[pltpu.VMEM((kept, 2 * per_chunk, side), f32)] * chunks,
        ],
        compiler_params=pltpu.CompilerParams(
            collective_id=0, has_side_effects=True, vmem_limit_bytes=64 * 1024 * 1024
        ),
        cost_estimate=pl.CostEstimate(flops=4_000_000, bytes_accessed=1_100_000, transcendentals=0),
        name="adjoint",
    )(*operands)
    return pl.pallas_call(
        hand_over,
        out_shape=tuple(jax.ShapeDtypeStruct(x.shape, x.dtype) for x in results),
        in_specs=[hbm] * 2,
        out_specs=(hbm, hbm),
        scratch_shapes=[
            *[pltpu.VMEM(x.shape, x.dtype) for x in results],
            pltpu.SemaphoreType.DMA((2, slots * PIECES + 1)),
        ],
        compiler_params=pltpu.CompilerParams(vmem_limit_bytes=64 * 1024 * 1024),
        name="hand_over",
    )(*results)


def solution(mesh):
    in_specs = (
        P(("basin", "blk"), None, None),
        P(("basin", "blk"), None, None),
        P(("basin", "blk"), None, None),
        P(("basin", "blk"), None),
        P(("basin", "blk")),
        P(None, ("basin", "blk")),
        P(("basin", "blk"), None, None, None),
        P(("basin", "blk"), None),
        P(("basin", "blk")),
        P(("basin", "blk")),
        P(),
    )
    out_specs = (P(("basin", "blk"), None, None), P(("basin", "blk")))
    return jax.shard_map(shards, mesh=mesh, in_specs=in_specs, out_specs=out_specs, check_vma=False)
```

```python
import functools

import jax
import jax.numpy as jnp
from jax import lax
from jax.experimental import pallas as pl
from jax.experimental.pallas import tpu as pltpu
from jax.sharding import PartitionSpec as P

coupling = 0.5
prior_weight = 0.5
MESH = pl.DeviceIdType.MESH
PAD = 8
PIECES = 4
PAIR = 2


def wrapped(value, count):
    return jnp.where(value >= count, value - count, value)


def split_exact(x):
    high = x.astype(jnp.bfloat16)
    left = x - high.astype(jnp.float32)
    middle = left.astype(jnp.bfloat16)
    return high, middle, (left - middle.astype(jnp.float32)).astype(jnp.bfloat16)


def weight_plan(steps, patterns):
    first = 0
    chunks = 1
    return first, chunks, -(-patterns // chunks)


def kernel(
    basins,
    groups,
    near_hbm,
    subfault_hbm,
    step_hbm,
    gauge_hbm,
    misfit_hbm,
    source_hbm,
    background_hbm,
    terminal_hbm,
    wet_hbm,
    depth_hbm,
    basis_hbm,
    surface_hbm,
    updated_ref,
    near_ref,
    subfault_ref,
    step_ref,
    gauge_ref,
    misfit_ref,
    source_ref,
    background_ref,
    terminal,
    wet,
    depth,
    basis,
    surface_ref,
    wet_f,
    wet_t,
    forces,
    early_across,
    early_along,
    late_across,
    late_along,
    turned_across,
    turned_along,
    across,
    along,
    across_md,
    along_md,
    across_flow,
    along_flow,
    edges,
    weights,
    sums_out,
    sums_in,
    chosen,
    load_sem,
    send_sem,
    recv_sem,
    sums_sem,
    *halo_buffers,
):
    slots, side, _ = terminal.shape
    steps = misfit_ref.shape[0]
    patterns = basis.shape[1]
    first_chunk, chunks, per_chunk = weight_plan(steps, patterns)
    outs, landings = halo_buffers[:steps], halo_buffers[steps : 2 * steps]
    weights_out = halo_buffers[2 * steps : 2 * steps + chunks]
    weights_in = halo_buffers[2 * steps + chunks :]
    owned = source_ref.shape[0]
    entries = slots * 4
    devices = basins * groups
    peers = 3 * groups
    basin = lax.axis_index("basin")
    group = lax.axis_index("blk")
    me = basin * groups + group

    pairs = (
        (near_hbm, near_ref),
        (subfault_hbm, subfault_ref),
        (step_hbm, step_ref),
        (gauge_hbm, gauge_ref),
        (misfit_hbm, misfit_ref),
        (source_hbm, source_ref),
        (background_hbm, background_ref),
        (terminal_hbm, terminal),
        (wet_hbm, wet),
        (depth_hbm, depth),
        (basis_hbm, basis),
    )
    loads = [pltpu.make_async_copy(a, b, load_sem.at[i]) for i, (a, b) in enumerate(pairs)]
    for load in loads:
        load.start()

    def each_peer(shifts, body):
        for shift in shifts:
            there = wrapped(basin + shift, basins)

            @pl.loop(1 if shift == 0 else 0, groups, unroll=min(groups, 8))
            def _(k):
                body(shift, there, wrapped(group + k, groups))

    barrier = pltpu.get_barrier_semaphore()

    def greet(shift, there, other):
        pl.semaphore_signal(barrier, inc=1, device_id=(there, other), device_id_type=MESH)

    each_peer(range(basins), greet)

    edges[...] = jnp.zeros_like(edges)

    loads[3].wait()
    loads[4].wait()
    gauge = gauge_ref[...].reshape(1, -1)
    count = gauge.shape[1]
    row_hot = lax.broadcasted_iota(jnp.int32, (slots * side, count), 0) == gauge // side
    row_hot = jnp.where(row_hot, 1.0, 0.0).astype(jnp.bfloat16)
    column_hot = lax.broadcasted_iota(jnp.int32, (side, count), 0) == gauge % side

    def injected(t):
        weights = jnp.where(column_hot, misfit_ref[t : t + 1, :], 0.0)
        total = None
        for part in split_exact(weights):
            term = lax.dot_general(
                row_hot, part, (((1,), (1,)), ((), ())), preferred_element_type=jnp.float32
            )
            total = term if total is None else total + term
        forces[...] = total.reshape(slots, side, side)

    injected(0)

    loads[0].wait()
    spare = peers * PAIR
    named = [near_ref[e // 4, e % 4] for e in range(entries)]
    present = [n >= 0 for n in named]
    safe = [jnp.maximum(n, 0) for n in named]
    holder = [n // slots for n in safe]
    origin = [safe[e] % slots * 4 + (e % 4) + 1 - 2 * (e % 2) for e in range(entries)]
    local = [h == me for h in holder]
    heading = [(h // groups - basin + 1 + basins) % basins for h in holder]
    place = [
        jnp.where(present[e], heading[e] * groups + holder[e] % groups, -1)
        for e in range(entries)
    ]
    @pl.loop(0, peers, unroll=8)
    def _(p):
        low = entries
        high = entries
        for e in range(entries):
            high = jnp.where(place[e] == p, e, high)
        for e in reversed(range(entries)):
            low = jnp.where(place[e] == p, e, low)
        chosen[p * PAIR] = low
        chosen[p * PAIR + 1] = high

    inside = slice(PAD, PAD + side)
    for load in loads[7:10]:
        load.wait()
    def await_bytes(ref, sem):
        pltpu.make_async_copy(ref, ref, sem).wait()

    for s in range(slots):
        m = wet[s].astype(jnp.float32)
        wet_f[s] = m
        md = m * depth[s] * (coupling * 0.5)
        along_md[s, inside] = md
        across_md[s, inside] = md.T
        masked = m * (terminal[s] + forces[s])
        along[s, inside] = masked
        across[s, inside] = masked.T

    ways = (
        (across, across_md, across_flow, wet_t, early_across, late_across, turned_along),
        (along, along_md, along_flow, wet_f, early_along, late_along, turned_across),
    )
    first, last = PAD, PAD + side - 1
    half = coupling * 0.5
    lane_row = lax.broadcasted_iota(jnp.int32, (1, side), 1)
    loads[1].wait()
    for s in range(slots):
        names = jnp.zeros((1, side), jnp.float32)
        for j in range(patterns):
            names = jnp.where(lane_row == j, subfault_ref[s, j].astype(jnp.float32), names)
        for w, (_, depths, *_) in enumerate(ways):
            low = s * 4 + 2 * w
            edges[low, 2:3] = depths[s, first : first + 1]
            edges[low + 1, 2:3] = depths[s, last : last + 1]
            for e in (low, low + 1):
                edges[e, 3:4] = names

    def pick(table, out, rows):
        for start in range(0, spare, 24):
            span = range(start, min(start + 24, spare))
            picked = [table[chosen[i], 0:rows] for i in span]
            for i, row in zip(span, picked):
                out[i] = row

    def keep_own(table, landing, rows):
        for e in range(entries + 1):
            landing[spare + e] = table[e, 0:rows]

    def send_all(out, landing, at_sem):
        def send(shift, there, other):
            at = (0 if shift == basins - 1 else shift + 1) * groups
            landing_at = (2 * groups - at + group) * PAIR
            pltpu.make_async_remote_copy(
                src_ref=out.at[pl.ds((at + other) * PAIR, PAIR)],
                dst_ref=landing.at[pl.ds(landing_at, PAIR)],
                send_sem=send_sem.at[at_sem],
                recv_sem=recv_sem.at[at_sem],
                device_id=(there, other),
                device_id_type=MESH,
            ).start()

        each_peer((1, basins - 1, 0), send)

    def send_weights(c):
        own = range(c * per_chunk, min((c + 1) * per_chunk, patterns))
        for s in range(slots):
            for i, j in enumerate(own):
                upright = basis[s, j]
                for w, (field, turned) in enumerate(((across_md, upright.T), (along_md, upright))):
                    low = s * 4 + 2 * w
                    for e, outer, inner, md_at in (
                        (low, 0, 1, first),
                        (low + 1, side - 1, side - 2, last),
                    ):
                        near = half * turned[inner : inner + 1] * field[s, md_at : md_at + 1]
                        weights[c, e, 2 * i : 2 * i + 1] = near
                        weights[c, e, 2 * i + 1 : 2 * i + 2] = half * turned[outer : outer + 1]
        pick(weights.at[c], weights_out[c], 2 * per_chunk)
        send_all(weights_out[c], weights_in[c], steps + c)
        keep_own(weights.at[c], weights_in[c], 2 * per_chunk)

    def partial_sums(facing):
        for c in range(chunks):
            await_bytes(weights_in[c].at[pl.ds(0, (peers - 1) * PAIR)], recv_sem.at[steps + c])
        lanes = sums_out.shape[2]
        row = lax.broadcasted_iota(jnp.int32, (devices, lanes), 0)
        lane = lax.broadcasted_iota(jnp.int32, (devices, lanes), 1)
        number = jnp.where(lane < owned, row * owned + lane, -1)
        number_f = number.astype(jnp.float32)
        shares = jnp.zeros((devices, lanes), jnp.float32)
        for s in range(slots):
            for j in range(patterns):
                down = jnp.sum(basis[s, j] * surface_ref[s], axis=0, keepdims=True)
                partial = jnp.sum(down, axis=1, keepdims=True)
                shares = shares + jnp.where(number == subfault_ref[s, j], partial, 0.0)
        odd = lax.broadcasted_iota(jnp.int32, (2 * per_chunk, side), 0) % 2 == 1
        for e in range(entries):
            near, far = (0, 1) if e % 2 == 0 else (1, 0)
            near_row = edges[e, near : near + 1]
            far_row = edges[e, far : far + 1] * edges[e, 2:3]
            for c in range(chunks):
                terms = weights_in[c][lookup[e]] * jnp.where(odd, far_row, near_row)
                dots = jnp.sum(terms, axis=1, keepdims=True)
                for i, j in enumerate(range(c * per_chunk, min((c + 1) * per_chunk, patterns))):
                    dot = dots[2 * i : 2 * i + 1] + dots[2 * i + 1 : 2 * i + 2]
                    shares = shares + jnp.where(number_f == facing[e][:, j : j + 1], dot, 0.0)
        sums_out[...] = shares.reshape(devices, 1, lanes)

    def send_sums():
        def send_sum(shift, there, other):
            target = there * groups + other
            pltpu.make_async_remote_copy(
                src_ref=sums_out.at[target],
                dst_ref=sums_in.at[me],
                send_sem=sums_sem.at[0],
                recv_sem=sums_sem.at[1],
                device_id=(there, other),
                device_id_type=MESH,
            ).start()

        each_peer([*range(1, basins), 0], send_sum)
        sums_in[me] = sums_out[me]

    rest = slice(PAD - 1, PAD + side + 1)
    before = slice(PAD - 2, PAD + side)
    after = slice(PAD, PAD + side + 2)
    facing = None
    outer_lanes = (0, 1, side - 2, side - 1)
    late_rows = {}
    for t in range(steps):
        out, landing = outs[t], landings[t]
        for s in range(slots):
            for w, (field, _, _, mask, early, late, turned) in enumerate(ways):
                for e, at in ((s * 4 + 2 * w, 0), (s * 4 + 2 * w + 1, side - 2)):
                    if t == 0:
                        edges[e, 0:2] = field[s, PAD + at : PAD + at + 2]
                    else:
                        for r in range(2):
                            y = at + r
                            own = late_rows[s, w][outer_lanes.index(y)]
                            crossing = jnp.zeros_like(own)
                            for x, other in zip(outer_lanes, late_rows[s, 1 - w]):
                                crossing = jnp.where(lane_row == x, other[:, y : y + 1], crossing)
                            edges[e, r : r + 1] = early[s, y : y + 1] + mask[s, y : y + 1] * (
                                own + crossing
                            )
        rows = 4 if t == 0 else 2
        pick(edges, out, rows)
        if t == 0:
            pl.semaphore_wait(barrier, devices - 1)
        send_all(out, landing, t)

        keep_own(edges, landing, rows)
        if t == 0:
            for ref in (across_flow, along_flow, late_across, late_along, weights):
                ref[...] = jnp.zeros_like(ref)
            for s in range(slots):
                wet_t[s] = wet_f[s].T
                for ref in (across, along, across_md, along_md):
                    ref[s, :PAD] = jnp.zeros((PAD, side), jnp.float32)
                    ref[s, PAD + side :] = jnp.zeros((PAD, side), jnp.float32)
            lookup = []
            for e in range(entries):
                rank = 0
                for f in range(entries):
                    if f != e:
                        earlier = (place[f] == place[e]) & (origin[f] < origin[e])
                        rank = jnp.where(earlier, 1, rank)
                index = jnp.where(local[e], spare + origin[e], place[e] * PAIR + rank)
                lookup.append(jnp.where(present[e], index, spare + entries))
            loads[10].wait()
        if first_chunk <= t < first_chunk + chunks:
            send_weights(t - first_chunk)
        if t + 1 < steps:
            injected(t + 1)
        for s in range(slots):
            if t > 0:
                turned_across[s] = late_across[s].T
                turned_along[s] = late_along[s].T
            for field, depths, flow, mask, early, late, turned in ways:
                if t > 0:
                    field[s, inside] = early[s] + mask[s] * (late[s] + turned[s])
                flow[s, rest] += depths[s, rest] * (field[s, after] - field[s, before])

            def gradient(flow):
                return half * (
                    flow[s, PAD + 1 : PAD + side + 1] - flow[s, PAD - 1 : PAD + side - 1]
                )

            surface = along[s, inside] + (gradient(across_flow).T + gradient(along_flow))
            if t + 1 < steps:
                masked = wet_f[s] * (surface + forces[s])
                early_along[s] = masked
                early_across[s] = masked.T
            else:
                surface_ref[s] = surface
        if t + 1 == steps:
            partial_sums(facing)
            send_sums()

        await_bytes(landing.at[pl.ds(0, (peers - 1) * PAIR)], recv_sem.at[t])
        fetched = [landing[lookup[e]] for e in range(entries)]
        if t == 0:
            facing = [got[3:4] for got in fetched]
        for s in range(slots):
            for w, (field, depths, flow, mask, early, late, turned) in enumerate(ways):
                low, high = fetched[s * 4 + 2 * w], fetched[s * 4 + 2 * w + 1]
                far_low, far_high = -low[0:1], high[1:2]
                if t == 0:
                    depths[s, first - 1 : first] = low[2:3]
                    depths[s, last + 1 : last + 2] = high[2:3]
                    far_low = field[s, first : first + 1] + far_low
                    far_high = far_high - field[s, last : last + 1]
                far_low = depths[s, first - 1 : first] * far_low
                near_low = -depths[s, first : first + 1] * low[1:2]
                near_high = depths[s, last : last + 1] * high[0:1]
                far_high = depths[s, last + 1 : last + 2] * far_high
                late_rows[s, w] = (
                    -half * far_low,
                    -half * near_low,
                    half * near_high,
                    half * far_high,
                )
                for y, late_row in zip(outer_lanes, late_rows[s, w]):
                    late[s, y : y + 1] = late_row
                if t + 1 < steps:
                    flow[s, first - 1 : first] += far_low
                    flow[s, first : first + 1] += near_low
                    flow[s, last : last + 1] += near_high
                    flow[s, last + 1 : last + 2] += far_high

    for s in range(slots):
        surface_ref[s] += late_along[s] + late_across[s].T
    store = pltpu.make_async_copy(surface_ref, surface_hbm, load_sem.at[len(pairs)])
    store.start()
    for load in (loads[2], loads[5], loads[6]):
        load.wait()
    source = source_ref[...].reshape(1, owned)
    background = background_ref[...].reshape(1, owned)
    prior = prior_weight * (source - background)
    await_bytes(sums_in.at[pl.ds(0, devices - 1)], sums_sem.at[1])
    mine = jnp.sum(sums_in[...], axis=0)[:, :owned]
    updated_ref[...] = (source - step_ref[0] * (prior + mine)).reshape(owned)
    store.wait()
    await_bytes(sums_out.at[pl.ds(0, devices - 1)], sums_sem.at[0])
    for t in range(steps):
        await_bytes(outs[t].at[pl.ds(0, (peers - 1) * PAIR)], send_sem.at[t])
    for c in range(chunks):
        await_bytes(weights_out[c].at[pl.ds(0, (peers - 1) * PAIR)], send_sem.at[steps + c])


def hand_over(surface, updated, surface_out, updated_out, surface_held, updated_held, sem):
    slots, side, _ = surface.shape
    size = side // PIECES
    moves = [(updated, updated_held, updated_out)]
    for s in range(slots):
        for i in range(PIECES):
            part = (s, pl.ds(i * size, size))
            moves.append((surface.at[part], surface_held.at[part], surface_out.at[part]))
    ins = [pltpu.make_async_copy(a, b, sem.at[0, i]) for i, (a, b, _) in enumerate(moves)]
    outs = [pltpu.make_async_copy(b, c, sem.at[1, i]) for i, (_, b, c) in enumerate(moves)]
    for copy in ins:
        copy.start()
    for arrived, copy in zip(ins, outs):
        arrived.wait()
        copy.start()
    for copy in outs:
        copy.wait()


def shards(
    terminal,
    depth,
    wet_cells,
    neighbours,
    gauge_cell,
    misfit,
    basis,
    subfault_index,
    source,
    background,
    step_size,
):
    slots, side, _ = terminal.shape
    steps = misfit.shape[0]
    patterns = basis.shape[1]
    first_chunk, chunks, per_chunk = weight_plan(steps, patterns)
    owned = source.shape[0]
    basins = lax.axis_size("basin")
    groups = lax.axis_size("blk")
    devices = basins * groups
    rows = 3 * groups * PAIR
    entries = slots * 4
    kept = rows + entries + 1
    lanes = -(-owned // 128) * 128
    widths = [4] + [2] * (steps - 1)
    f32 = jnp.float32
    padded = pltpu.VMEM((slots, side + 2 * PAD, side), f32)
    vmem = pl.BlockSpec(memory_space=pltpu.VMEM)
    hbm = pl.BlockSpec(memory_space=pltpu.HBM)
    scalars = (neighbours, subfault_index, step_size)
    vectors = (
        gauge_cell,
        misfit,
        source,
        background,
        terminal,
        wet_cells,
        depth,
        basis,
    )
    operands = scalars + vectors
    results = pl.pallas_call(
        functools.partial(kernel, basins, groups),
        out_shape=(
            jax.ShapeDtypeStruct(terminal.shape, f32),
            jax.ShapeDtypeStruct(source.shape, f32),
        ),
        in_specs=[hbm] * len(operands),
        out_specs=(hbm, vmem),
        scratch_shapes=[
            *[pltpu.SMEM(x.shape, x.dtype) for x in scalars],
            *[pltpu.VMEM(x.shape, x.dtype) for x in vectors],
            *[pltpu.VMEM(terminal.shape, f32)] * 10,
            padded,
            padded,
            padded,
            padded,
            padded,
            padded,
            pltpu.VMEM((entries + 1, 4, side), f32),
            pltpu.VMEM((chunks, entries + 1, 2 * per_chunk, side), f32),
            pltpu.VMEM((devices, 1, lanes), f32),
            pltpu.VMEM((devices, 1, lanes), f32),
            pltpu.SMEM((rows,), jnp.int32),
            pltpu.SemaphoreType.DMA((len(operands) + 1,)),
            pltpu.SemaphoreType.DMA((steps + chunks,)),
            pltpu.SemaphoreType.DMA((steps + chunks,)),
            pltpu.SemaphoreType.DMA((2,)),
            *[pltpu.VMEM((rows, width, side), f32) for width in widths],
            *[pltpu.VMEM((kept, width, side), f32) for width in widths],
            *[pltpu.VMEM((rows, 2 * per_chunk, side), f32)] * chunks,
            *[pltpu.VMEM((kept, 2 * per_chunk, side), f32)] * chunks,
        ],
        compiler_params=pltpu.CompilerParams(
            collective_id=0, has_side_effects=True, vmem_limit_bytes=64 * 1024 * 1024
        ),
        cost_estimate=pl.CostEstimate(flops=4_000_000, bytes_accessed=1_100_000, transcendentals=0),
        name="adjoint",
    )(*operands)
    return pl.pallas_call(
        hand_over,
        out_shape=tuple(jax.ShapeDtypeStruct(x.shape, x.dtype) for x in results),
        in_specs=[hbm] * 2,
        out_specs=(hbm, hbm),
        scratch_shapes=[
            *[pltpu.VMEM(x.shape, x.dtype) for x in results],
            pltpu.SemaphoreType.DMA((2, slots * PIECES + 1)),
        ],
        compiler_params=pltpu.CompilerParams(vmem_limit_bytes=64 * 1024 * 1024),
        name="hand_over",
    )(*results)


def solution(mesh):
    in_specs = (
        P(("basin", "blk"), None, None),
        P(("basin", "blk"), None, None),
        P(("basin", "blk"), None, None),
        P(("basin", "blk"), None),
        P(("basin", "blk")),
        P(None, ("basin", "blk")),
        P(("basin", "blk"), None, None, None),
        P(("basin", "blk"), None),
        P(("basin", "blk")),
        P(("basin", "blk")),
        P(),
    )
    out_specs = (P(("basin", "blk"), None, None), P(("basin", "blk")))
    return jax.shard_map(shards, mesh=mesh, in_specs=in_specs, out_specs=out_specs, check_vma=False)
```

```python
import functools

import jax
import jax.numpy as jnp
from jax import lax
from jax.experimental import pallas as pl
from jax.experimental.pallas import tpu as pltpu
from jax.sharding import PartitionSpec as P

coupling = 0.5
prior_weight = 0.5
MESH = pl.DeviceIdType.MESH
PAD = 8
PIECES = 4
PAIR = 2


def wrapped(value, count):
    return jnp.where(value >= count, value - count, value)


def split_exact(x):
    high = x.astype(jnp.bfloat16)
    left = x - high.astype(jnp.float32)
    middle = left.astype(jnp.bfloat16)
    return high, middle, (left - middle.astype(jnp.float32)).astype(jnp.bfloat16)


def weight_plan(steps, patterns):
    first = 0
    chunks = 1
    return first, chunks, -(-patterns // chunks)


def kernel(
    basins,
    groups,
    near_hbm,
    subfault_hbm,
    step_hbm,
    gauge_hbm,
    misfit_hbm,
    source_hbm,
    background_hbm,
    terminal_hbm,
    wet_hbm,
    depth_hbm,
    basis_hbm,
    surface_hbm,
    updated_ref,
    near_ref,
    subfault_ref,
    step_ref,
    gauge_ref,
    misfit_ref,
    source_ref,
    background_ref,
    terminal,
    wet,
    depth,
    basis,
    surface_ref,
    wet_f,
    wet_t,
    forces,
    early_across,
    early_along,
    late_across,
    late_along,
    turned_across,
    turned_along,
    across,
    along,
    across_md,
    along_md,
    across_flow,
    along_flow,
    edges,
    weights,
    sums_out,
    sums_in,
    chosen,
    load_sem,
    send_sem,
    recv_sem,
    sums_sem,
    *halo_buffers,
):
    slots, side, _ = terminal.shape
    steps = misfit_ref.shape[0]
    patterns = basis.shape[1]
    first_chunk, chunks, per_chunk = weight_plan(steps, patterns)
    outs, landings = halo_buffers[:steps], halo_buffers[steps : 2 * steps]
    weights_out = halo_buffers[2 * steps : 2 * steps + chunks]
    weights_in = halo_buffers[2 * steps + chunks :]
    owned = source_ref.shape[0]
    entries = slots * 4
    devices = basins * groups
    peers = 3 * groups
    basin = lax.axis_index("basin")
    group = lax.axis_index("blk")
    me = basin * groups + group

    pairs = (
        (near_hbm, near_ref),
        (subfault_hbm, subfault_ref),
        (step_hbm, step_ref),
        (gauge_hbm, gauge_ref),
        (misfit_hbm, misfit_ref),
        (source_hbm, source_ref),
        (background_hbm, background_ref),
        (terminal_hbm, terminal),
        (wet_hbm, wet),
        (depth_hbm, depth),
        (basis_hbm, basis),
    )
    loads = [pltpu.make_async_copy(a, b, load_sem.at[i]) for i, (a, b) in enumerate(pairs)]
    def each_peer(shifts, body):
        for shift in shifts:
            there = wrapped(basin + shift, basins)

            @pl.loop(1 if shift == 0 else 0, groups, unroll=min(groups, 8))
            def _(k):
                body(shift, there, wrapped(group + k, groups))

    barrier = pltpu.get_barrier_semaphore()

    def greet(shift, there, other):
        pl.semaphore_signal(barrier, inc=1, device_id=(there, other), device_id_type=MESH)

    each_peer(range(basins), greet)
    for load in loads:
        load.start()

    edges[...] = jnp.zeros_like(edges)

    loads[3].wait()
    loads[4].wait()
    gauge = gauge_ref[...].reshape(1, -1)
    count = gauge.shape[1]
    row_hot = lax.broadcasted_iota(jnp.int32, (slots * side, count), 0) == gauge // side
    row_hot = jnp.where(row_hot, 1.0, 0.0).astype(jnp.bfloat16)
    column_hot = lax.broadcasted_iota(jnp.int32, (side, count), 0) == gauge % side

    def injected(t):
        weights = jnp.where(column_hot, misfit_ref[t : t + 1, :], 0.0)
        total = None
        for part in split_exact(weights):
            term = lax.dot_general(
                row_hot, part, (((1,), (1,)), ((), ())), preferred_element_type=jnp.float32
            )
            total = term if total is None else total + term
        forces[...] = total.reshape(slots, side, side)

    injected(0)

    loads[0].wait()
    spare = peers * PAIR
    named = [near_ref[e // 4, e % 4] for e in range(entries)]
    present = [n >= 0 for n in named]
    safe = [jnp.maximum(n, 0) for n in named]
    holder = [n // slots for n in safe]
    origin = [safe[e] % slots * 4 + (e % 4) + 1 - 2 * (e % 2) for e in range(entries)]
    local = [h == me for h in holder]
    heading = [(h // groups - basin + 1 + basins) % basins for h in holder]
    place = [
        jnp.where(present[e], heading[e] * groups + holder[e] % groups, -1)
        for e in range(entries)
    ]
    @pl.loop(0, peers, unroll=8)
    def _(p):
        low = entries
        high = entries
        for e in range(entries):
            high = jnp.where(place[e] == p, e, high)
        for e in reversed(range(entries)):
            low = jnp.where(place[e] == p, e, low)
        chosen[p * PAIR] = low
        chosen[p * PAIR + 1] = high

    inside = slice(PAD, PAD + side)
    for load in loads[7:10]:
        load.wait()
    def await_bytes(ref, sem):
        pltpu.make_async_copy(ref, ref, sem).wait()

    for s in range(slots):
        m = wet[s].astype(jnp.float32)
        wet_f[s] = m
        md = m * depth[s] * (coupling * 0.5)
        along_md[s, inside] = md
        across_md[s, inside] = md.T
        masked = m * (terminal[s] + forces[s])
        along[s, inside] = masked
        across[s, inside] = masked.T

    ways = (
        (across, across_md, across_flow, wet_t, early_across, late_across, turned_along),
        (along, along_md, along_flow, wet_f, early_along, late_along, turned_across),
    )
    first, last = PAD, PAD + side - 1
    half = coupling * 0.5
    lane_row = lax.broadcasted_iota(jnp.int32, (1, side), 1)
    loads[1].wait()
    for s in range(slots):
        names = jnp.zeros((1, side), jnp.float32)
        for j in range(patterns):
            names = jnp.where(lane_row == j, subfault_ref[s, j].astype(jnp.float32), names)
        for w, (_, depths, *_) in enumerate(ways):
            low = s * 4 + 2 * w
            edges[low, 2:3] = depths[s, first : first + 1]
            edges[low + 1, 2:3] = depths[s, last : last + 1]
            for e in (low, low + 1):
                edges[e, 3:4] = names

    def pick(table, out, rows):
        for start in range(0, spare, 24):
            span = range(start, min(start + 24, spare))
            picked = [table[chosen[i], 0:rows] for i in span]
            for i, row in zip(span, picked):
                out[i] = row

    def keep_own(table, landing, rows):
        for e in range(entries + 1):
            landing[spare + e] = table[e, 0:rows]

    def send_all(out, landing, at_sem):
        def send(shift, there, other):
            at = (0 if shift == basins - 1 else shift + 1) * groups
            landing_at = (2 * groups - at + group) * PAIR
            pltpu.make_async_remote_copy(
                src_ref=out.at[pl.ds((at + other) * PAIR, PAIR)],
                dst_ref=landing.at[pl.ds(landing_at, PAIR)],
                send_sem=send_sem.at[at_sem],
                recv_sem=recv_sem.at[at_sem],
                device_id=(there, other),
                device_id_type=MESH,
            ).start()

        each_peer((1, basins - 1, 0), send)

    def send_weights(c):
        own = range(c * per_chunk, min((c + 1) * per_chunk, patterns))
        for s in range(slots):
            for i, j in enumerate(own):
                upright = basis[s, j]
                for w, (field, turned) in enumerate(((across_md, upright.T), (along_md, upright))):
                    low = s * 4 + 2 * w
                    for e, outer, inner, md_at in (
                        (low, 0, 1, first),
                        (low + 1, side - 1, side - 2, last),
                    ):
                        near = half * turned[inner : inner + 1] * field[s, md_at : md_at + 1]
                        weights[c, e, 2 * i : 2 * i + 1] = near
                        weights[c, e, 2 * i + 1 : 2 * i + 2] = half * turned[outer : outer + 1]
        pick(weights.at[c], weights_out[c], 2 * per_chunk)
        send_all(weights_out[c], weights_in[c], steps + c)
        keep_own(weights.at[c], weights_in[c], 2 * per_chunk)

    def halo_sums(facing):
        lanes = sums_out.shape[2]
        row = lax.broadcasted_iota(jnp.int32, (devices, lanes), 0)
        lane = lax.broadcasted_iota(jnp.int32, (devices, lanes), 1)
        number = jnp.where(lane < owned, row * owned + lane, -1)
        number_f = number.astype(jnp.float32)
        shares = jnp.zeros((devices, lanes), jnp.float32)
        odd = lax.broadcasted_iota(jnp.int32, (2 * per_chunk, side), 0) % 2 == 1
        for e in range(entries):
            near, far = (0, 1) if e % 2 == 0 else (1, 0)
            near_row = edges[e, near : near + 1]
            far_row = edges[e, far : far + 1] * edges[e, 2:3]
            for c in range(chunks):
                terms = weights_in[c][lookup[e]] * jnp.where(odd, far_row, near_row)
                dots = jnp.sum(terms, axis=1, keepdims=True)
                for i, j in enumerate(range(c * per_chunk, min((c + 1) * per_chunk, patterns))):
                    dot = dots[2 * i : 2 * i + 1] + dots[2 * i + 1 : 2 * i + 2]
                    shares = shares + jnp.where(number_f == facing[e][:, j : j + 1], dot, 0.0)
        return number, shares

    def partial_sums(number, shares):
        for s in range(slots):
            for j in range(patterns):
                down = jnp.sum(basis[s, j] * surface_ref[s], axis=0, keepdims=True)
                partial = jnp.sum(down, axis=1, keepdims=True)
                shares = shares + jnp.where(number == subfault_ref[s, j], partial, 0.0)
        sums_out[...] = shares.reshape(sums_out.shape)

    def send_sums():
        def send_sum(shift, there, other):
            target = there * groups + other
            pltpu.make_async_remote_copy(
                src_ref=sums_out.at[target],
                dst_ref=sums_in.at[me],
                send_sem=sums_sem.at[0],
                recv_sem=sums_sem.at[1],
                device_id=(there, other),
                device_id_type=MESH,
            ).start()

        each_peer([*range(1, basins), 0], send_sum)
        sums_in[me] = sums_out[me]

    rest = slice(PAD - 1, PAD + side + 1)
    before = slice(PAD - 2, PAD + side)
    after = slice(PAD, PAD + side + 2)
    facing = None
    outer_lanes = (0, 1, side - 2, side - 1)
    late_rows = {}
    for t in range(steps):
        out, landing = outs[t], landings[t]
        for s in range(slots):
            for w, (field, _, _, mask, early, late, turned) in enumerate(ways):
                for e, at in ((s * 4 + 2 * w, 0), (s * 4 + 2 * w + 1, side - 2)):
                    if t == 0:
                        edges[e, 0:2] = field[s, PAD + at : PAD + at + 2]
                    else:
                        for r in range(2):
                            y = at + r
                            own = late_rows[s, w][outer_lanes.index(y)]
                            crossing = jnp.zeros_like(own)
                            for x, other in zip(outer_lanes, late_rows[s, 1 - w]):
                                crossing = jnp.where(lane_row == x, other[:, y : y + 1], crossing)
                            edges[e, r : r + 1] = early[s, y : y + 1] + mask[s, y : y + 1] * (
                                own + crossing
                            )
        rows = 4 if t == 0 else 2
        pick(edges, out, rows)
        if t + 1 == steps:
            for c in range(chunks):
                landed = weights_in[c].at[pl.ds(0, (peers - 1) * PAIR)]
                await_bytes(landed, recv_sem.at[steps + c])
        if t == 0:
            pl.semaphore_wait(barrier, devices - 1)
        send_all(out, landing, t)

        keep_own(edges, landing, rows)
        if t == 0:
            for ref in (across_flow, along_flow, late_across, late_along, weights):
                ref[...] = jnp.zeros_like(ref)
            for s in range(slots):
                wet_t[s] = wet_f[s].T
                for ref in (across, along, across_md, along_md):
                    ref[s, :PAD] = jnp.zeros((PAD, side), jnp.float32)
                    ref[s, PAD + side :] = jnp.zeros((PAD, side), jnp.float32)
            lookup = []
            for e in range(entries):
                rank = 0
                for f in range(entries):
                    if f != e:
                        earlier = (place[f] == place[e]) & (origin[f] < origin[e])
                        rank = jnp.where(earlier, 1, rank)
                index = jnp.where(local[e], spare + origin[e], place[e] * PAIR + rank)
                lookup.append(jnp.where(present[e], index, spare + entries))
            loads[10].wait()
        if first_chunk <= t < first_chunk + chunks:
            send_weights(t - first_chunk)
        if t + 1 < steps:
            injected(t + 1)
        else:
            crossing_sums = halo_sums(facing)
        for s in range(slots):
            if t > 0:
                turned_across[s] = late_across[s].T
                turned_along[s] = late_along[s].T
            for field, depths, flow, mask, early, late, turned in ways:
                if t > 0:
                    field[s, inside] = early[s] + mask[s] * (late[s] + turned[s])
                flow[s, rest] += depths[s, rest] * (field[s, after] - field[s, before])

            def gradient(flow):
                return half * (
                    flow[s, PAD + 1 : PAD + side + 1] - flow[s, PAD - 1 : PAD + side - 1]
                )

            surface = along[s, inside] + (gradient(across_flow).T + gradient(along_flow))
            if t + 1 < steps:
                masked = wet_f[s] * (surface + forces[s])
                early_along[s] = masked
                early_across[s] = masked.T
            else:
                surface_ref[s] = surface
        if t + 1 == steps:
            partial_sums(*crossing_sums)
            send_sums()

        await_bytes(landing.at[pl.ds(0, (peers - 1) * PAIR)], recv_sem.at[t])
        fetched = [landing[lookup[e]] for e in range(entries)]
        if t == 0:
            facing = [got[3:4] for got in fetched]
        for s in range(slots):
            for w, (field, depths, flow, mask, early, late, turned) in enumerate(ways):
                low, high = fetched[s * 4 + 2 * w], fetched[s * 4 + 2 * w + 1]
                far_low, far_high = -low[0:1], high[1:2]
                if t == 0:
                    depths[s, first - 1 : first] = low[2:3]
                    depths[s, last + 1 : last + 2] = high[2:3]
                    far_low = field[s, first : first + 1] + far_low
                    far_high = far_high - field[s, last : last + 1]
                far_low = depths[s, first - 1 : first] * far_low
                near_low = -depths[s, first : first + 1] * low[1:2]
                near_high = depths[s, last : last + 1] * high[0:1]
                far_high = depths[s, last + 1 : last + 2] * far_high
                late_rows[s, w] = (
                    -half * far_low,
                    -half * near_low,
                    half * near_high,
                    half * far_high,
                )
                for y, late_row in zip(outer_lanes, late_rows[s, w]):
                    late[s, y : y + 1] = late_row
                if t + 1 < steps:
                    flow[s, first - 1 : first] += far_low
                    flow[s, first : first + 1] += near_low
                    flow[s, last : last + 1] += near_high
                    flow[s, last + 1 : last + 2] += far_high

    for s in range(slots):
        surface_ref[s] += late_along[s] + late_across[s].T
    store = pltpu.make_async_copy(surface_ref, surface_hbm, load_sem.at[len(pairs)])
    store.start()
    for load in (loads[2], loads[5], loads[6]):
        load.wait()
    source = source_ref[...].reshape(1, owned)
    background = background_ref[...].reshape(1, owned)
    prior = prior_weight * (source - background)
    await_bytes(sums_in.at[pl.ds(0, devices - 1)], sums_sem.at[1])
    mine = jnp.sum(sums_in[...], axis=0)[:, :owned]
    updated_ref[...] = (source - step_ref[0] * (prior + mine)).reshape(owned)
    store.wait()
    await_bytes(sums_out.at[pl.ds(0, devices - 1)], sums_sem.at[0])
    for t in range(steps):
        await_bytes(outs[t].at[pl.ds(0, (peers - 1) * PAIR)], send_sem.at[t])
    for c in range(chunks):
        await_bytes(weights_out[c].at[pl.ds(0, (peers - 1) * PAIR)], send_sem.at[steps + c])


def hand_over(surface, updated, surface_out, updated_out, surface_held, updated_held, sem):
    slots, side, _ = surface.shape
    size = side // PIECES
    moves = [(updated, updated_held, updated_out)]
    for s in range(slots):
        for i in range(PIECES):
            part = (s, pl.ds(i * size, size))
            moves.append((surface.at[part], surface_held.at[part], surface_out.at[part]))
    ins = [pltpu.make_async_copy(a, b, sem.at[0, i]) for i, (a, b, _) in enumerate(moves)]
    outs = [pltpu.make_async_copy(b, c, sem.at[1, i]) for i, (_, b, c) in enumerate(moves)]
    for copy in ins:
        copy.start()
    for arrived, copy in zip(ins, outs):
        arrived.wait()
        copy.start()
    for copy in outs:
        copy.wait()


def shards(
    terminal,
    depth,
    wet_cells,
    neighbours,
    gauge_cell,
    misfit,
    basis,
    subfault_index,
    source,
    background,
    step_size,
):
    slots, side, _ = terminal.shape
    steps = misfit.shape[0]
    patterns = basis.shape[1]
    first_chunk, chunks, per_chunk = weight_plan(steps, patterns)
    owned = source.shape[0]
    basins = lax.axis_size("basin")
    groups = lax.axis_size("blk")
    devices = basins * groups
    rows = 3 * groups * PAIR
    entries = slots * 4
    kept = rows + entries + 1
    lanes = -(-owned // 128) * 128
    widths = [4] + [2] * (steps - 1)
    f32 = jnp.float32
    padded = pltpu.VMEM((slots, side + 2 * PAD, side), f32)
    vmem = pl.BlockSpec(memory_space=pltpu.VMEM)
    hbm = pl.BlockSpec(memory_space=pltpu.HBM)
    scalars = (neighbours, subfault_index, step_size)
    vectors = (
        gauge_cell,
        misfit,
        source,
        background,
        terminal,
        wet_cells,
        depth,
        basis,
    )
    operands = scalars + vectors
    results = pl.pallas_call(
        functools.partial(kernel, basins, groups),
        out_shape=(
            jax.ShapeDtypeStruct(terminal.shape, f32),
            jax.ShapeDtypeStruct(source.shape, f32),
        ),
        in_specs=[hbm] * len(operands),
        out_specs=(hbm, vmem),
        scratch_shapes=[
            *[pltpu.SMEM(x.shape, x.dtype) for x in scalars],
            *[pltpu.VMEM(x.shape, x.dtype) for x in vectors],
            *[pltpu.VMEM(terminal.shape, f32)] * 10,
            padded,
            padded,
            padded,
            padded,
            padded,
            padded,
            pltpu.VMEM((entries + 1, 4, side), f32),
            pltpu.VMEM((chunks, entries + 1, 2 * per_chunk, side), f32),
            pltpu.VMEM((devices, 1, lanes), f32),
            pltpu.VMEM((devices, 1, lanes), f32),
            pltpu.SMEM((rows,), jnp.int32),
            pltpu.SemaphoreType.DMA((len(operands) + 1,)),
            pltpu.SemaphoreType.DMA((steps + chunks,)),
            pltpu.SemaphoreType.DMA((steps + chunks,)),
            pltpu.SemaphoreType.DMA((2,)),
            *[pltpu.VMEM((rows, width, side), f32) for width in widths],
            *[pltpu.VMEM((kept, width, side), f32) for width in widths],
            *[pltpu.VMEM((rows, 2 * per_chunk, side), f32)] * chunks,
            *[pltpu.VMEM((kept, 2 * per_chunk, side), f32)] * chunks,
        ],
        compiler_params=pltpu.CompilerParams(
            collective_id=0, has_side_effects=True, vmem_limit_bytes=64 * 1024 * 1024
        ),
        cost_estimate=pl.CostEstimate(flops=4_000_000, bytes_accessed=1_100_000, transcendentals=0),
        name="adjoint",
    )(*operands)
    return pl.pallas_call(
        hand_over,
        out_shape=tuple(jax.ShapeDtypeStruct(x.shape, x.dtype) for x in results),
        in_specs=[hbm] * 2,
        out_specs=(hbm, hbm),
        scratch_shapes=[
            *[pltpu.VMEM(x.shape, x.dtype) for x in results],
            pltpu.SemaphoreType.DMA((2, slots * PIECES + 1)),
        ],
        compiler_params=pltpu.CompilerParams(vmem_limit_bytes=64 * 1024 * 1024),
        name="hand_over",
    )(*results)


def solution(mesh):
    in_specs = (
        P(("basin", "blk"), None, None),
        P(("basin", "blk"), None, None),
        P(("basin", "blk"), None, None),
        P(("basin", "blk"), None),
        P(("basin", "blk")),
        P(None, ("basin", "blk")),
        P(("basin", "blk"), None, None, None),
        P(("basin", "blk"), None),
        P(("basin", "blk")),
        P(("basin", "blk")),
        P(),
    )
    out_specs = (P(("basin", "blk"), None, None), P(("basin", "blk")))
    return jax.shard_map(shards, mesh=mesh, in_specs=in_specs, out_specs=out_specs, check_vma=False)
```

```python
import functools

import jax
import jax.numpy as jnp
from jax import lax
from jax.experimental import pallas as pl
from jax.experimental.pallas import tpu as pltpu
from jax.sharding import PartitionSpec as P

coupling = 0.5
prior_weight = 0.5
MESH = pl.DeviceIdType.MESH
PAD = 8
PIECES = 4
PAIR = 2


def wrapped(value, count):
    return jnp.where(value >= count, value - count, value)


def split_exact(x):
    high = x.astype(jnp.bfloat16)
    left = x - high.astype(jnp.float32)
    middle = left.astype(jnp.bfloat16)
    return high, middle, (left - middle.astype(jnp.float32)).astype(jnp.bfloat16)


def weight_plan(steps, patterns):
    first = 0
    chunks = 1
    return first, chunks, -(-patterns // chunks)


def kernel(
    basins,
    groups,
    near_hbm,
    subfault_hbm,
    step_hbm,
    gauge_hbm,
    misfit_hbm,
    source_hbm,
    background_hbm,
    terminal_hbm,
    wet_hbm,
    depth_hbm,
    basis_hbm,
    surface_hbm,
    updated_ref,
    near_ref,
    subfault_ref,
    step_ref,
    gauge_ref,
    misfit_ref,
    source_ref,
    background_ref,
    terminal,
    wet,
    depth,
    basis,
    surface_ref,
    wet_f,
    wet_t,
    forces,
    early_across,
    early_along,
    late_across,
    late_along,
    turned_across,
    turned_along,
    across,
    along,
    across_md,
    along_md,
    across_flow,
    along_flow,
    edges,
    weights,
    sums_out,
    sums_in,
    chosen,
    load_sem,
    send_sem,
    recv_sem,
    sums_sem,
    *halo_buffers,
):
    slots, side, _ = terminal.shape
    steps = misfit_ref.shape[0]
    patterns = basis.shape[1]
    first_chunk, chunks, per_chunk = weight_plan(steps, patterns)
    outs, landings = halo_buffers[:steps], halo_buffers[steps : 2 * steps]
    weights_out = halo_buffers[2 * steps : 2 * steps + chunks]
    weights_in = halo_buffers[2 * steps + chunks :]
    owned = source_ref.shape[0]
    entries = slots * 4
    devices = basins * groups
    peers = 3 * groups
    basin = lax.axis_index("basin")
    group = lax.axis_index("blk")
    me = basin * groups + group

    pairs = (
        (near_hbm, near_ref),
        (subfault_hbm, subfault_ref),
        (step_hbm, step_ref),
        (gauge_hbm, gauge_ref),
        (misfit_hbm, misfit_ref),
        (source_hbm, source_ref),
        (background_hbm, background_ref),
        (terminal_hbm, terminal),
        (wet_hbm, wet),
        (depth_hbm, depth),
        (basis_hbm, basis),
    )
    loads = [pltpu.make_async_copy(a, b, load_sem.at[i]) for i, (a, b) in enumerate(pairs)]
    for load in loads:
        load.start()

    def each_peer(shifts, body):
        for shift in shifts:
            there = wrapped(basin + shift, basins)

            @pl.loop(1 if shift == 0 else 0, groups, unroll=min(groups, 8))
            def _(k):
                body(shift, there, wrapped(group + k, groups))

    barrier = pltpu.get_barrier_semaphore()

    def greet(shift, there, other):
        pl.semaphore_signal(barrier, inc=1, device_id=(there, other), device_id_type=MESH)

    each_peer(range(basins), greet)

    edges[...] = jnp.zeros_like(edges)

    loads[3].wait()
    loads[4].wait()
    gauge = gauge_ref[...].reshape(1, -1)
    count = gauge.shape[1]
    row_hot = lax.broadcasted_iota(jnp.int32, (slots * side, count), 0) == gauge // side
    row_hot = jnp.where(row_hot, 1.0, 0.0).astype(jnp.bfloat16)
    column_hot = lax.broadcasted_iota(jnp.int32, (side, count), 0) == gauge % side

    def injected(t):
        weights = jnp.where(column_hot, misfit_ref[t : t + 1, :], 0.0)
        total = None
        for part in split_exact(weights):
            term = lax.dot_general(
                row_hot, part, (((1,), (1,)), ((), ())), preferred_element_type=jnp.float32
            )
            total = term if total is None else total + term
        forces[...] = total.reshape(slots, side, side)

    injected(0)

    loads[0].wait()
    spare = peers * PAIR
    named = [near_ref[e // 4, e % 4] for e in range(entries)]
    present = [n >= 0 for n in named]
    safe = [jnp.maximum(n, 0) for n in named]
    holder = [n // slots for n in safe]
    origin = [safe[e] % slots * 4 + (e % 4) + 1 - 2 * (e % 2) for e in range(entries)]
    local = [h == me for h in holder]
    heading = [(h // groups - basin + 1 + basins) % basins for h in holder]
    place = [
        jnp.where(present[e], heading[e] * groups + holder[e] % groups, -1)
        for e in range(entries)
    ]
    @pl.loop(0, peers, unroll=8)
    def _(p):
        low = entries
        high = entries
        for e in range(entries):
            high = jnp.where(place[e] == p, e, high)
        for e in reversed(range(entries)):
            low = jnp.where(place[e] == p, e, low)
        chosen[p * PAIR] = low
        chosen[p * PAIR + 1] = high

    inside = slice(PAD, PAD + side)
    for load in loads[7:10]:
        load.wait()
    def await_bytes(ref, sem):
        pltpu.make_async_copy(ref, ref, sem).wait()

    for s in range(slots):
        m = wet[s].astype(jnp.float32)
        wet_f[s] = m
        md = m * depth[s] * (coupling * 0.5)
        along_md[s, inside] = md
        across_md[s, inside] = md.T
        masked = m * (terminal[s] + forces[s])
        along[s, inside] = masked
        across[s, inside] = masked.T

    ways = (
        (across, across_md, across_flow, wet_t, early_across, late_across, turned_along),
        (along, along_md, along_flow, wet_f, early_along, late_along, turned_across),
    )
    first, last = PAD, PAD + side - 1
    half = coupling * 0.5
    lane_row = lax.broadcasted_iota(jnp.int32, (1, side), 1)
    loads[1].wait()
    for s in range(slots):
        names = jnp.zeros((1, side), jnp.float32)
        for j in range(patterns):
            names = jnp.where(lane_row == j, subfault_ref[s, j].astype(jnp.float32), names)
        for w, (_, depths, *_) in enumerate(ways):
            low = s * 4 + 2 * w
            edges[low, 2:3] = depths[s, first : first + 1]
            edges[low + 1, 2:3] = depths[s, last : last + 1]
            for e in (low, low + 1):
                edges[e, 3:4] = names

    def pick(table, out, rows, low, high):
        for start in range(low, high, 24):
            span = range(start, min(start + 24, high))
            picked = [table[chosen[i], 0:rows] for i in span]
            for i, row in zip(span, picked):
                out[i] = row

    def keep_own(table, landing, rows):
        for e in range(entries + 1):
            landing[spare + e] = table[e, 0:rows]

    def send_all(table, rows, out, landing, at_sem):
        def send(shift, there, other):
            at = (0 if shift == basins - 1 else shift + 1) * groups
            landing_at = (2 * groups - at + group) * PAIR
            pltpu.make_async_remote_copy(
                src_ref=out.at[pl.ds((at + other) * PAIR, PAIR)],
                dst_ref=landing.at[pl.ds(landing_at, PAIR)],
                send_sem=send_sem.at[at_sem],
                recv_sem=recv_sem.at[at_sem],
                device_id=(there, other),
                device_id_type=MESH,
            ).start()

        for shift, at in ((1, 2 * groups), (basins - 1, 0), (0, groups)):
            pick(table, out, rows, at * PAIR, (at + groups) * PAIR)
            each_peer((shift,), send)

    def send_weights(c):
        own = range(c * per_chunk, min((c + 1) * per_chunk, patterns))
        for s in range(slots):
            for i, j in enumerate(own):
                upright = basis[s, j]
                for w, (field, turned) in enumerate(((across_md, upright.T), (along_md, upright))):
                    low = s * 4 + 2 * w
                    for e, outer, inner, md_at in (
                        (low, 0, 1, first),
                        (low + 1, side - 1, side - 2, last),
                    ):
                        near = half * turned[inner : inner + 1] * field[s, md_at : md_at + 1]
                        weights[c, e, 2 * i : 2 * i + 1] = near
                        weights[c, e, 2 * i + 1 : 2 * i + 2] = half * turned[outer : outer + 1]
        send_all(weights.at[c], 2 * per_chunk, weights_out[c], weights_in[c], steps + c)
        keep_own(weights.at[c], weights_in[c], 2 * per_chunk)

    def partial_sums(facing):
        for c in range(chunks):
            await_bytes(weights_in[c].at[pl.ds(0, (peers - 1) * PAIR)], recv_sem.at[steps + c])
        lanes = sums_out.shape[2]
        row = lax.broadcasted_iota(jnp.int32, (devices, lanes), 0)
        lane = lax.broadcasted_iota(jnp.int32, (devices, lanes), 1)
        number = jnp.where(lane < owned, row * owned + lane, -1)
        number_f = number.astype(jnp.float32)
        shares = jnp.zeros((devices, lanes), jnp.float32)
        for s in range(slots):
            for j in range(patterns):
                down = jnp.sum(basis[s, j] * surface_ref[s], axis=0, keepdims=True)
                partial = jnp.sum(down, axis=1, keepdims=True)
                shares = shares + jnp.where(number == subfault_ref[s, j], partial, 0.0)
        odd = lax.broadcasted_iota(jnp.int32, (2 * per_chunk, side), 0) % 2 == 1
        for e in range(entries):
            near, far = (0, 1) if e % 2 == 0 else (1, 0)
            near_row = edges[e, near : near + 1]
            far_row = edges[e, far : far + 1] * edges[e, 2:3]
            for c in range(chunks):
                terms = weights_in[c][lookup[e]] * jnp.where(odd, far_row, near_row)
                dots = jnp.sum(terms, axis=1, keepdims=True)
                for i, j in enumerate(range(c * per_chunk, min((c + 1) * per_chunk, patterns))):
                    dot = dots[2 * i : 2 * i + 1] + dots[2 * i + 1 : 2 * i + 2]
                    shares = shares + jnp.where(number_f == facing[e][:, j : j + 1], dot, 0.0)
        sums_out[...] = shares.reshape(devices, 1, lanes)

    def send_sums():
        def send_sum(shift, there, other):
            target = there * groups + other
            pltpu.make_async_remote_copy(
                src_ref=sums_out.at[target],
                dst_ref=sums_in.at[me],
                send_sem=sums_sem.at[0],
                recv_sem=sums_sem.at[1],
                device_id=(there, other),
                device_id_type=MESH,
            ).start()

        each_peer([*range(1, basins), 0], send_sum)
        sums_in[me] = sums_out[me]

    rest = slice(PAD - 1, PAD + side + 1)
    before = slice(PAD - 2, PAD + side)
    after = slice(PAD, PAD + side + 2)
    facing = None
    outer_lanes = (0, 1, side - 2, side - 1)
    late_rows = {}
    for t in range(steps):
        out, landing = outs[t], landings[t]
        for s in range(slots):
            for w, (field, _, _, mask, early, late, turned) in enumerate(ways):
                for e, at in ((s * 4 + 2 * w, 0), (s * 4 + 2 * w + 1, side - 2)):
                    if t == 0:
                        edges[e, 0:2] = field[s, PAD + at : PAD + at + 2]
                    else:
                        for r in range(2):
                            y = at + r
                            own = late_rows[s, w][outer_lanes.index(y)]
                            crossing = jnp.zeros_like(own)
                            for x, other in zip(outer_lanes, late_rows[s, 1 - w]):
                                crossing = jnp.where(lane_row == x, other[:, y : y + 1], crossing)
                            edges[e, r : r + 1] = early[s, y : y + 1] + mask[s, y : y + 1] * (
                                own + crossing
                            )
        rows = 4 if t == 0 else 2
        if t == 0:
            pl.semaphore_wait(barrier, devices - 1)
        send_all(edges, rows, out, landing, t)

        keep_own(edges, landing, rows)
        if t == 0:
            for ref in (across_flow, along_flow, late_across, late_along, weights):
                ref[...] = jnp.zeros_like(ref)
            for s in range(slots):
                wet_t[s] = wet_f[s].T
                for ref in (across, along, across_md, along_md):
                    ref[s, :PAD] = jnp.zeros((PAD, side), jnp.float32)
                    ref[s, PAD + side :] = jnp.zeros((PAD, side), jnp.float32)
            lookup = []
            for e in range(entries):
                rank = 0
                for f in range(entries):
                    if f != e:
                        earlier = (place[f] == place[e]) & (origin[f] < origin[e])
                        rank = jnp.where(earlier, 1, rank)
                index = jnp.where(local[e], spare + origin[e], place[e] * PAIR + rank)
                lookup.append(jnp.where(present[e], index, spare + entries))
            loads[10].wait()
        if first_chunk <= t < first_chunk + chunks:
            send_weights(t - first_chunk)
        if t + 1 < steps:
            injected(t + 1)
        for s in range(slots):
            if t > 0:
                turned_across[s] = late_across[s].T
                turned_along[s] = late_along[s].T
            for field, depths, flow, mask, early, late, turned in ways:
                if t > 0:
                    field[s, inside] = early[s] + mask[s] * (late[s] + turned[s])
                flow[s, rest] += depths[s, rest] * (field[s, after] - field[s, before])

            def gradient(flow):
                return half * (
                    flow[s, PAD + 1 : PAD + side + 1] - flow[s, PAD - 1 : PAD + side - 1]
                )

            surface = along[s, inside] + (gradient(across_flow).T + gradient(along_flow))
            if t + 1 < steps:
                masked = wet_f[s] * (surface + forces[s])
                early_along[s] = masked
                early_across[s] = masked.T
            else:
                surface_ref[s] = surface
        if t + 1 == steps:
            partial_sums(facing)
            send_sums()

        await_bytes(landing.at[pl.ds(0, (peers - 1) * PAIR)], recv_sem.at[t])
        fetched = [landing[lookup[e]] for e in range(entries)]
        if t == 0:
            facing = [got[3:4] for got in fetched]
        for s in range(slots):
            for w, (field, depths, flow, mask, early, late, turned) in enumerate(ways):
                low, high = fetched[s * 4 + 2 * w], fetched[s * 4 + 2 * w + 1]
                far_low, far_high = -low[0:1], high[1:2]
                if t == 0:
                    depths[s, first - 1 : first] = low[2:3]
                    depths[s, last + 1 : last + 2] = high[2:3]
                    far_low = field[s, first : first + 1] + far_low
                    far_high = far_high - field[s, last : last + 1]
                far_low = depths[s, first - 1 : first] * far_low
                near_low = -depths[s, first : first + 1] * low[1:2]
                near_high = depths[s, last : last + 1] * high[0:1]
                far_high = depths[s, last + 1 : last + 2] * far_high
                late_rows[s, w] = (
                    -half * far_low,
                    -half * near_low,
                    half * near_high,
                    half * far_high,
                )
                for y, late_row in zip(outer_lanes, late_rows[s, w]):
                    late[s, y : y + 1] = late_row
                if t + 1 < steps:
                    flow[s, first - 1 : first] += far_low
                    flow[s, first : first + 1] += near_low
                    flow[s, last : last + 1] += near_high
                    flow[s, last + 1 : last + 2] += far_high

    for s in range(slots):
        surface_ref[s] += late_along[s] + late_across[s].T
    store = pltpu.make_async_copy(surface_ref, surface_hbm, load_sem.at[len(pairs)])
    store.start()
    for load in (loads[2], loads[5], loads[6]):
        load.wait()
    source = source_ref[...].reshape(1, owned)
    background = background_ref[...].reshape(1, owned)
    prior = prior_weight * (source - background)
    await_bytes(sums_in.at[pl.ds(0, devices - 1)], sums_sem.at[1])
    mine = jnp.sum(sums_in[...], axis=0)[:, :owned]
    updated_ref[...] = (source - step_ref[0] * (prior + mine)).reshape(owned)
    store.wait()
    await_bytes(sums_out.at[pl.ds(0, devices - 1)], sums_sem.at[0])
    for t in range(steps):
        await_bytes(outs[t].at[pl.ds(0, (peers - 1) * PAIR)], send_sem.at[t])
    for c in range(chunks):
        await_bytes(weights_out[c].at[pl.ds(0, (peers - 1) * PAIR)], send_sem.at[steps + c])


def hand_over(surface, updated, surface_out, updated_out, surface_held, updated_held, sem):
    slots, side, _ = surface.shape
    size = side // PIECES
    moves = [(updated, updated_held, updated_out)]
    for s in range(slots):
        for i in range(PIECES):
            part = (s, pl.ds(i * size, size))
            moves.append((surface.at[part], surface_held.at[part], surface_out.at[part]))
    ins = [pltpu.make_async_copy(a, b, sem.at[0, i]) for i, (a, b, _) in enumerate(moves)]
    outs = [pltpu.make_async_copy(b, c, sem.at[1, i]) for i, (_, b, c) in enumerate(moves)]
    for copy in ins:
        copy.start()
    for arrived, copy in zip(ins, outs):
        arrived.wait()
        copy.start()
    for copy in outs:
        copy.wait()


def shards(
    terminal,
    depth,
    wet_cells,
    neighbours,
    gauge_cell,
    misfit,
    basis,
    subfault_index,
    source,
    background,
    step_size,
):
    slots, side, _ = terminal.shape
    steps = misfit.shape[0]
    patterns = basis.shape[1]
    first_chunk, chunks, per_chunk = weight_plan(steps, patterns)
    owned = source.shape[0]
    basins = lax.axis_size("basin")
    groups = lax.axis_size("blk")
    devices = basins * groups
    rows = 3 * groups * PAIR
    entries = slots * 4
    kept = rows + entries + 1
    lanes = -(-owned // 128) * 128
    widths = [4] + [2] * (steps - 1)
    f32 = jnp.float32
    padded = pltpu.VMEM((slots, side + 2 * PAD, side), f32)
    vmem = pl.BlockSpec(memory_space=pltpu.VMEM)
    hbm = pl.BlockSpec(memory_space=pltpu.HBM)
    scalars = (neighbours, subfault_index, step_size)
    vectors = (
        gauge_cell,
        misfit,
        source,
        background,
        terminal,
        wet_cells,
        depth,
        basis,
    )
    operands = scalars + vectors
    results = pl.pallas_call(
        functools.partial(kernel, basins, groups),
        out_shape=(
            jax.ShapeDtypeStruct(terminal.shape, f32),
            jax.ShapeDtypeStruct(source.shape, f32),
        ),
        in_specs=[hbm] * len(operands),
        out_specs=(hbm, vmem),
        scratch_shapes=[
            *[pltpu.SMEM(x.shape, x.dtype) for x in scalars],
            *[pltpu.VMEM(x.shape, x.dtype) for x in vectors],
            *[pltpu.VMEM(terminal.shape, f32)] * 10,
            padded,
            padded,
            padded,
            padded,
            padded,
            padded,
            pltpu.VMEM((entries + 1, 4, side), f32),
            pltpu.VMEM((chunks, entries + 1, 2 * per_chunk, side), f32),
            pltpu.VMEM((devices, 1, lanes), f32),
            pltpu.VMEM((devices, 1, lanes), f32),
            pltpu.SMEM((rows,), jnp.int32),
            pltpu.SemaphoreType.DMA((len(operands) + 1,)),
            pltpu.SemaphoreType.DMA((steps + chunks,)),
            pltpu.SemaphoreType.DMA((steps + chunks,)),
            pltpu.SemaphoreType.DMA((2,)),
            *[pltpu.VMEM((rows, width, side), f32) for width in widths],
            *[pltpu.VMEM((kept, width, side), f32) for width in widths],
            *[pltpu.VMEM((rows, 2 * per_chunk, side), f32)] * chunks,
            *[pltpu.VMEM((kept, 2 * per_chunk, side), f32)] * chunks,
        ],
        compiler_params=pltpu.CompilerParams(
            collective_id=0, has_side_effects=True, vmem_limit_bytes=64 * 1024 * 1024
        ),
        cost_estimate=pl.CostEstimate(flops=4_000_000, bytes_accessed=1_100_000, transcendentals=0),
        name="adjoint",
    )(*operands)
    return pl.pallas_call(
        hand_over,
        out_shape=tuple(jax.ShapeDtypeStruct(x.shape, x.dtype) for x in results),
        in_specs=[hbm] * 2,
        out_specs=(hbm, hbm),
        scratch_shapes=[
            *[pltpu.VMEM(x.shape, x.dtype) for x in results],
            pltpu.SemaphoreType.DMA((2, slots * PIECES + 1)),
        ],
        compiler_params=pltpu.CompilerParams(vmem_limit_bytes=64 * 1024 * 1024),
        name="hand_over",
    )(*results)


def solution(mesh):
    in_specs = (
        P(("basin", "blk"), None, None),
        P(("basin", "blk"), None, None),
        P(("basin", "blk"), None, None),
        P(("basin", "blk"), None),
        P(("basin", "blk")),
        P(None, ("basin", "blk")),
        P(("basin", "blk"), None, None, None),
        P(("basin", "blk"), None),
        P(("basin", "blk")),
        P(("basin", "blk")),
        P(),
    )
    out_specs = (P(("basin", "blk"), None, None), P(("basin", "blk")))
    return jax.shard_map(shards, mesh=mesh, in_specs=in_specs, out_specs=out_specs, check_vma=False)
```
